32 devices in a mesh: group: 8 (over y, x, core), head: 4 (over z).
Axes of the slice: x: 2, y: 2, z: 4, core: 2. Of those that a mesh axis runs over, the one named last changes fastest.
Arguments:
- key_grad: bfloat16 [4096, 16384], P('group', 'head'), may hold values from -6 to 6
- value_grad: bfloat16 [4096, 16384], P('group', 'head'), may hold values from -6 to 6
- rope_grad: bfloat16 [4096, 8192], P('group', 'head'), may hold values from -1.5 to 1.5
- key_lift: bfloat16 [512, 16384], P(None, 'head'), may hold values from -0.046875 to 0.046875
- value_lift: bfloat16 [512, 16384], P(None, 'head'), may hold values from -0.046875 to 0.046875
- latent: bfloat16 [4096, 512], P('group'), may hold values from -40 to 40
- norm_gain: float32 [512], replicated, may hold values from 0.25 to 1.75
- doc_lengths: int32 [8, 4], P('group'), may hold values from 1 to 256, 512 in all within a row
- hidden: bfloat16 [4096, 7168], P('group', 'head'), may hold values from -0.25 to 0.25
- down_proj: bfloat16 [7168, 576], P('head'), may hold values from -0.0625 to 0.0625
Outputs:
- hidden_grad: bfloat16 [4096, 7168], P('group', 'head')
- weight_grad: float32 [576, 7168], P('group', 'head')
The draws below stay inside these ranges and needn't reach their ends.
Inputs may be any that keep to these rules, and one draw needn't show every extreme that they name: `doc_lengths`: each row sums to 512 and its largest entry is 256.
All inputs are finite; a program needn't handle non-finite values.
Results may differ from the reference program's by a relative error of at most 0.0049.
Values may be sent and summed in bfloat16 or wider, within the bound.
No kernel may reach another device: no remote copies, remote signals or barrier semaphores. Data moves between devices by JAX's collectives and lax.ppermute only.
A program may use at most 64 MiB of HBM per device.

```python
import math
import jax
import jax.numpy as jnp
import numpy as np
from jax import lax

D = 7168
HEADS = 128
HD = 128
VD = 128
LATENT = 512
ROPE = 64
SEQ = 512
DOCS = 4
KVW = 576
TOKENS = 4096
MOST_DOC = 256
N_GROUP = 8


def draw_latent(key, part):
    first_key, second_key = jax.random.split(key, 2)
    row_scale = jnp.exp(jax.random.uniform(second_key, (TOKENS, 1), jnp.float32, 0.0, math.log(10.0)))
    base = jnp.clip(jax.random.normal(first_key, (TOKENS, LATENT), jnp.float32), -4.0, 4.0)
    values = base * row_scale
    return values.astype(jnp.bfloat16)


def spiked(result, key, source, target, parts, factor):
    def block_of(dim):
        return (jnp.arange(result.shape[dim]) // (result.shape[dim] // parts)).reshape((-1,) + (1,) * (result.ndim - 1 - dim))

    first = jax.random.permutation(key, parts)[block_of(target)]
    other_side = (block_of(target) + parts // 2) % parts
    return jnp.where((block_of(source) == first) | (block_of(source) == other_side), factor * result, result)


def level_of(stream_key, dims, cuts, smallest, high):
    gain, own = 1.0, jax.random.fold_in(stream_key, 6)
    for dim, shards_of in cuts:
        steps = jnp.exp(jax.random.uniform(jax.random.fold_in(own, dim), (shards_of,), jnp.float32, smallest / len(cuts), high / len(cuts)))
        gain = gain * jnp.repeat(steps, dims[dim] // shards_of).reshape([-1 if axis == dim else 1 for axis in range(len(dims))])
    return gain


def split_up(amount, total, limit, lean):
    loads = [(1 << 20) // math.isqrt(rank ** lean) + 1 for rank in range(2, amount + 1)]
    rest, given = total - limit - (amount - 1), [1] * (amount - 1)
    while rest > 0:
        movable = [i for i in range(amount - 1) if given[i] < limit]
        whole, budget = sum([loads[i] for i in movable]), rest
        for i in movable:
            addition = min(limit - given[i], max(1, budget * loads[i] // whole), rest)
            given[i] = given[i] + addition
            rest = rest - addition
    return np.array([limit] + given)


def uneven_parts(own_key, count, total, limit, skew):
    if count == 2:
        one = jax.random.randint(own_key, (), max(1, total - limit), min(limit, total - 1) + 1)
        return jnp.stack([one, total - one])
    sizes = jnp.asarray(split_up(count, total, limit, skew), jnp.int32)
    pairs = (count - 1) // 2
    source_of, taker = sizes[1:1 + 2 * pairs:2], sizes[2:2 + 2 * pairs:2]
    slack = jnp.minimum(source_of - 1, limit - taker)
    passed = jax.random.randint(jax.random.fold_in(own_key, 1), (pairs,), 0, 1 << 20) % (slack + 1)
    sizes = sizes.at[1:1 + 2 * pairs:2].set(source_of - passed).at[2:2 + 2 * pairs:2].set(taker + passed)
    return sizes[jax.random.permutation(jax.random.fold_in(own_key, 2), count)]


def centred(rng, shape, scale, limit, pieces=(), kind=jnp.bfloat16):
    result = jax.random.normal(rng, shape, jnp.float32) * scale
    if len(pieces) > 0:
        result = level_of(rng, shape, pieces, -0.22, 0.18) * result
    return jnp.clip(result, min=-limit, max=limit).astype(kind)


def heavy_noise(stream_key, dims, spread, reach, cuts, heavy, kind=jnp.bfloat16):
    entries = spread * jax.random.normal(stream_key, dims, jnp.float32)
    if cuts:
        entries = entries * level_of(stream_key, dims, cuts, -0.22, 0.18)
    return jnp.clip(spiked(entries, jax.random.fold_in(stream_key, 3), *heavy), -reach, reach).astype(kind)


def setup_inputs(seed: int = 0) -> dict:
    splits = jax.random.split(jax.random.key(seed), 11)
    key_grad = heavy_noise(splits[0], (TOKENS, HEADS * HD), 1.0, 6.0, ((0, 8), (1, 4)), (1, 0, 8, 2.0))
    value_grad = centred(splits[1], (TOKENS, HEADS * VD), 1.0, 6.0, ((0, 8), (1, 4)))
    rope_grad = centred(splits[2], (TOKENS, HEADS * ROPE), 0.1, 1.5, ((0, 8), (1, 4)))
    key_lift = centred(splits[3], (LATENT, HEADS * HD), (HEADS * HD) ** -0.5, 0.046875, ((1, 4),))
    value_lift = centred(splits[4], (LATENT, HEADS * VD), (HEADS * VD) ** -0.5, 0.046875, ((1, 4),))
    latent = draw_latent(jax.random.fold_in(splits[10], 71), 0)
    norm_gain = jnp.clip(1.0 + 0.15 * jax.random.normal(splits[6], (LATENT,), jnp.float32), 0.25, 1.75)
    doc_lengths = jax.vmap(lambda own: uneven_parts(own, DOCS, SEQ, MOST_DOC, 2))(jax.random.split(splits[7], N_GROUP)).reshape((N_GROUP, DOCS)).astype(jnp.int32)
    hidden = centred(splits[8], (TOKENS, D), (TOKENS ** -0.5), 0.25, ((0, 8), (1, 4)))
    down_proj = centred(splits[9], (D, KVW), D ** -0.5, 0.0625, ((0, 4),))
    return {"key_grad": key_grad, "value_grad": value_grad, "rope_grad": rope_grad, "key_lift": key_lift, "value_lift": value_lift, "latent": latent, "norm_gain": norm_gain, "doc_lengths": doc_lengths, "hidden": hidden, "down_proj": down_proj}


def positions(lengths, token_index):
    doc_ends = jnp.cumsum(lengths, axis=1).astype(jnp.int32)
    doc_start = lax.optimization_barrier(jnp.max(jnp.where(doc_ends <= token_index[:, None], doc_ends, 0), axis=1))
    return (token_index - doc_start).astype(jnp.int32)

def kva_rows_grad(stacked, latent, norm_gain, position):
    latent_part = stacked[:, :LATENT]
    rotary_part = stacked[:, LATENT:]
    values = latent.astype(jnp.float32)
    inverse_rms = lax.rsqrt(lax.optimization_barrier(jnp.mean(values * values, axis=1, keepdims=True)) + 1e-06)
    scaled_grad = latent_part * norm_gain[None, :]
    norm_grad = inverse_rms * (scaled_grad - values * inverse_rms * inverse_rms * lax.optimization_barrier(jnp.mean(scaled_grad * values, axis=1, keepdims=True)))
    half_width = rotary_part.shape[1] // 2
    inv_freq = 10000.0 ** (-(2.0 * jnp.arange(half_width, dtype=jnp.float32)) / (2.0 * half_width))
    angles = position.astype(jnp.float32)[:, None] * inv_freq[None, :]
    cosine = jnp.cos(angles)
    sine = jnp.sin(angles)
    first_half = rotary_part[:, :half_width]
    second_half = rotary_part[:, half_width:]
    rot_first = first_half * cosine + second_half * sine
    rot_second = second_half * cosine - first_half * sine
    return jnp.concatenate([norm_grad, rot_first, rot_second], axis=1).astype(jnp.bfloat16)

def reference(key_grad, value_grad, rope_grad, key_lift, value_lift, latent, norm_gain, doc_lengths, hidden, down_proj):
    latent_sum = jnp.dot(key_grad, key_lift.T, preferred_element_type=jnp.float32)
    latent_sum = latent_sum + jnp.dot(value_grad, value_lift.T, preferred_element_type=jnp.float32)
    tokens_all = key_grad.shape[0]
    rope_sum = lax.optimization_barrier(jnp.sum(rope_grad.reshape(tokens_all, HEADS, ROPE), axis=1, dtype=jnp.float32))
    stacked = jnp.concatenate([latent_sum, rope_sum], axis=1)
    token_ids = jnp.arange(tokens_all, dtype=jnp.int32)
    row_lengths = doc_lengths[(token_ids // SEQ).astype(jnp.int32)]
    position = positions(row_lengths, (token_ids % SEQ).astype(jnp.int32))
    kva_grad = kva_rows_grad(stacked, latent, norm_gain, position)
    hidden_grad = jnp.dot(kva_grad, down_proj.T, preferred_element_type=jnp.float32).astype(jnp.bfloat16)
    weight_grad = jnp.dot(kva_grad.T, hidden, preferred_element_type=jnp.float32)
    return (hidden_grad, weight_grad)
```

```python
import functools

import jax
import jax.numpy as jnp
import numpy as np
from jax import lax
from jax.experimental import pallas as pl
from jax.experimental.pallas import tpu as pltpu
from jax.sharding import PartitionSpec as P

F32 = jnp.float32
BF16 = jnp.bfloat16
LAST = (((1,), (1,)), ((), ()))
FIRST = (((0,), (0,)), ((), ()))
MIB = 1 << 20


def positions(lengths, token_index):
    doc_ends = jnp.cumsum(lengths, axis=1)
    doc_start = jnp.max(jnp.where(doc_ends <= token_index[:, None], doc_ends, 0), axis=1)
    return token_index - doc_start


def kva_rows_grad(stacked, latent, norm_gain, position):
    width = latent.shape[1]
    latent_part = stacked[:, :width]
    rotary_part = stacked[:, width:]
    values = latent.astype(F32)
    inverse_rms = lax.rsqrt(jnp.mean(values * values, axis=1, keepdims=True) + 1e-06)
    scaled_grad = latent_part * norm_gain[None, :]
    norm_grad = inverse_rms * (
        scaled_grad
        - values * inverse_rms * inverse_rms * jnp.mean(scaled_grad * values, axis=1, keepdims=True)
    )
    half_width = rotary_part.shape[1] // 2
    inv_freq = 10000.0 ** (-(2.0 * jnp.arange(half_width, dtype=F32)) / (2.0 * half_width))
    angles = position.astype(F32)[:, None] * inv_freq[None, :]
    cosine = jnp.cos(angles)
    sine = jnp.sin(angles)
    first_half = rotary_part[:, :half_width]
    second_half = rotary_part[:, half_width:]
    rot_first = first_half * cosine + second_half * sine
    rot_second = second_half * cosine - first_half * sine
    return jnp.concatenate([norm_grad, rot_first, rot_second], axis=1).astype(BF16)


def on_device_any(
    key_grad, value_grad, rope_grad, key_lift, value_lift, latent, norm_gain, doc_lengths, hidden, down_proj
):
    seq_len = key_grad.shape[0]
    rope = down_proj.shape[1] - latent.shape[1]
    head_terms = lax.dot_general(key_grad, key_lift, LAST, preferred_element_type=F32)
    head_terms = head_terms + lax.dot_general(value_grad, value_lift, LAST, preferred_element_type=F32)
    heads_here = rope_grad.shape[1] // rope
    rope_terms = jnp.sum(rope_grad.reshape(seq_len, heads_here, rope), axis=1, dtype=F32)
    stacked = jnp.concatenate([head_terms, rope_terms], axis=1)
    shared = lax.psum_scatter(stacked, "head", scatter_dimension=0, tiled=True)
    share_rows = shared.shape[0]
    first_row = lax.axis_index("head") * share_rows
    own_latent = lax.dynamic_slice_in_dim(latent, first_row, share_rows, 0)
    token_index = first_row + jnp.arange(share_rows, dtype=jnp.int32)
    row_lengths = jnp.broadcast_to(doc_lengths, (share_rows, doc_lengths.shape[1]))
    own_grad = kva_rows_grad(shared, own_latent, norm_gain, positions(row_lengths, token_index))
    kva_grad = lax.all_gather(own_grad, "head", axis=0, tiled=True)
    hidden_grad = lax.dot_general(kva_grad, down_proj, LAST, preferred_element_type=F32).astype(BF16)
    weight_grad = lax.psum_scatter(
        lax.dot_general(kva_grad, hidden, FIRST, preferred_element_type=F32),
        "group",
        scatter_dimension=0,
        tiled=True,
    )
    return (hidden_grad, weight_grad)


def partial_kernel(
    index, lengths,
    kg_a, kg_b, vg_a, vg_b, rg_a, rg_b, kl, vl, lat_a, lat_b, gain, freq,
    out_a, out_b, acc, rope_acc, values, rows,
    *, which, block,
):
    step = pl.program_id(0)
    share = kg_a.shape[0]
    rope = rope_acc.shape[0]
    latent = acc.shape[0]

    @pl.when(step == 0)
    def _():
        acc[...] = jnp.zeros_like(acc)
        rope_acc[...] = jnp.zeros_like(rope_acc)
        values[:, :share] = lat_a[...].astype(F32).T
        values[:, share:] = lat_b[...].astype(F32).T

    keys = jnp.concatenate([kg_a[...], kg_b[...]], axis=0)
    vals = jnp.concatenate([vg_a[...], vg_b[...]], axis=0)
    acc[...] += lax.dot_general(kl[...], keys, LAST, preferred_element_type=F32) + lax.dot_general(
        vl[...], vals, LAST, preferred_element_type=F32
    )
    ropes = jnp.concatenate([rg_a[...], rg_b[...]], axis=0)
    fold_shape = (rope, ropes.shape[1])
    fold = lax.rem(lax.broadcasted_iota(jnp.int32, fold_shape, 1), rope) == lax.broadcasted_iota(
        jnp.int32, fold_shape, 0
    )
    rope_acc[...] += lax.dot_general(fold.astype(BF16), ropes, LAST, preferred_element_type=F32)

    @pl.when(step == pl.num_programs(0) - 1)
    def _():
        gains = jnp.broadcast_to(gain[...], (share, latent)).T
        half = rope // 2
        lane = lax.broadcasted_iota(jnp.int32, (1, share), 1)
        for side in range(2):
            lanes = slice(side * share, (side + 1) * share)
            c = values[:, lanes]
            inv = lax.rsqrt(jnp.mean(c * c, axis=0, keepdims=True) + 1e-06)
            g = acc[:, lanes] * gains
            mean = jnp.mean(g * c, axis=0, keepdims=True)
            rows[:latent, lanes] = inv * (g - c * (inv * inv * mean))
            token = index[which[side]] * share + lane
            start = jnp.zeros_like(token)
            end = jnp.int32(0)
            for doc in range(lengths.shape[1]):
                end = end + lengths[0, doc]
                start = jnp.maximum(start, jnp.where(end <= token, end, 0))
            angle = (token - start).astype(F32) * freq[...]
            cosine, sine = jnp.cos(angle), jnp.sin(angle)
            first, second = rope_acc[:half, lanes], rope_acc[half:, lanes]
            rows[latent : latent + half, lanes] = first * cosine + second * sine
            rows[latent + half :, lanes] = second * cosine - first * sine
        blocks = rows.shape[0] // block
        ordered = jnp.concatenate(
            [rows[pl.ds(pl.multiple_of(index[4 + i] * block, 8), block), :] for i in range(blocks)], axis=0
        )
        out_a[...] = ordered[:, :share].astype(out_a.dtype)
        out_b[...] = ordered[:, share:].astype(out_b.dtype)


def partial_terms(which, out_dtype, index, doc_lengths, kg, vg, rg, kl, vl, latent, gain, freq, share, block):
    tokens, key_cols = kg.shape
    width = latent.shape[1]
    rope = 2 * freq.shape[0]
    kva = width + rope
    steps = max(1, key_cols // 512)
    key_block, rope_block = key_cols // steps, rg.shape[1] // steps
    a, b = which

    def grad_spec(cols, side):
        return pl.BlockSpec((share, cols), lambda k, ix, ln: (ix[side], k))

    def lift_spec():
        return pl.BlockSpec((width, key_block), lambda k, ix, ln: (0, k))

    def latent_spec(side):
        return pl.BlockSpec((share, width), lambda k, ix, ln: (ix[side], 0))

    def whole(shape):
        return pl.BlockSpec(shape, lambda k, ix, ln: (0,) * len(shape))

    return pl.pallas_call(
        functools.partial(partial_kernel, which=which, block=block),
        grid_spec=pltpu.PrefetchScalarGridSpec(
            num_scalar_prefetch=2,
            grid=(steps,),
            in_specs=[
                grad_spec(key_block, a), grad_spec(key_block, b),
                grad_spec(key_block, a), grad_spec(key_block, b),
                grad_spec(rope_block, a), grad_spec(rope_block, b),
                lift_spec(), lift_spec(),
                latent_spec(a), latent_spec(b),
                whole((1, width)), whole(freq.shape),
            ],
            out_specs=[whole((kva, share))] * 2,
            scratch_shapes=[
                pltpu.VMEM((width, 2 * share), F32),
                pltpu.VMEM((rope, 2 * share), F32),
                pltpu.VMEM((width, 2 * share), F32),
                pltpu.VMEM((kva, 2 * share), F32),
            ],
        ),
        out_shape=[jax.ShapeDtypeStruct((kva, share), out_dtype)] * 2,
        compiler_params=pltpu.CompilerParams(vmem_limit_bytes=24 * MIB),
        cost_estimate=pl.CostEstimate(
            flops=2 * 2 * share * width * key_cols * 2,
            bytes_accessed=2 * (2 * width * key_cols + 2 * share * (2 * key_cols + rg.shape[1])),
            transcendentals=0,
        ),
        name="partial_terms",
    )(index, doc_lengths, kg, kg, vg, vg, rg, rg, kl, vl, latent, latent, gain, freq)


def weight_kernel(index, *refs):
    own, sibling, own_hidden, sibling_hidden = refs[:4], refs[4:8], refs[8:12], refs[12:16]
    send, keep = refs[16:18]
    half = own[0].shape[0] // 2
    left = jnp.concatenate([r[:half] for r in own] + [r[half:] for r in sibling], axis=1)
    right = jnp.concatenate([r[...] for r in own_hidden] + [r[...] for r in sibling_hidden], axis=0)
    result = jnp.dot(left, right, preferred_element_type=F32)
    send[...] = result[: half // 2].astype(send.dtype)
    keep[...] = result[half // 2 :]


def weight_terms(index, own, sibling, hidden, sibling_hidden):
    kva, share = own[0].shape
    columns = hidden.shape[1]
    col_block = columns // 2 if columns % 256 == 0 else columns
    quarter = kva // 4

    def hidden_spec(r):
        return pl.BlockSpec((share, col_block), lambda n, ix: (ix[r], n))

    whole = pl.BlockSpec((kva, share), lambda n, ix: (0, 0))
    out = pl.BlockSpec((quarter, col_block), lambda n, ix: (0, n))
    return pl.pallas_call(
        weight_kernel,
        grid_spec=pltpu.PrefetchScalarGridSpec(
            num_scalar_prefetch=1,
            grid=(columns // col_block,),
            in_specs=[whole] * 8 + [hidden_spec(r) for r in range(4)] * 2,
            out_specs=[out, out],
        ),
        out_shape=[
            jax.ShapeDtypeStruct((quarter, columns), BF16),
            jax.ShapeDtypeStruct((quarter, columns), F32),
        ],
        compiler_params=pltpu.CompilerParams(vmem_limit_bytes=32 * MIB),
        cost_estimate=pl.CostEstimate(
            flops=2 * (kva // 2) * 8 * share * columns, bytes_accessed=8 * MIB, transcendentals=0
        ),
        name="weight_terms",
    )(index, *own, *sibling, *([hidden] * 4), *([sibling_hidden] * 4))


def hidden_kernel(index, q0, q1, q2, q3, down_t, out, kva, natural, *, block):
    share = q0.shape[1]

    @pl.when(pl.program_id(0) == 0)
    def _():
        for r, q in enumerate((q0, q1, q2, q3)):
            ordered = q[...].astype(F32)
            for i in range(ordered.shape[0] // block):
                natural[pl.ds(pl.multiple_of(index[4 + i] * block, 8), block), :] = ordered[
                    i * block : (i + 1) * block
                ]
            kva[pl.ds(pl.multiple_of(index[r] * share, 128), share), :] = natural[...].T.astype(BF16)

    out[...] = jnp.dot(kva[...], down_t[...], preferred_element_type=F32).astype(out.dtype)


def hidden_terms(index, gathered, down_t, block):
    kva, share = gathered[0].shape
    columns = down_t.shape[1]
    col_block = columns // 2 if columns % 256 == 0 else columns
    tokens = 4 * share
    whole = pl.BlockSpec((kva, share), lambda n, ix: (0, 0))
    return pl.pallas_call(
        functools.partial(hidden_kernel, block=block),
        grid_spec=pltpu.PrefetchScalarGridSpec(
            num_scalar_prefetch=1,
            grid=(columns // col_block,),
            in_specs=[whole] * 4 + [pl.BlockSpec((kva, col_block), lambda n, ix: (0, n))],
            out_specs=pl.BlockSpec((tokens, col_block), lambda n, ix: (0, n)),
            scratch_shapes=[pltpu.VMEM((tokens, kva), BF16), pltpu.VMEM((kva, share), F32)],
        ),
        out_shape=jax.ShapeDtypeStruct((tokens, columns), BF16),
        compiler_params=pltpu.CompilerParams(vmem_limit_bytes=32 * MIB),
        cost_estimate=pl.CostEstimate(
            flops=2 * tokens * kva * columns, bytes_accessed=5 * MIB, transcendentals=0
        ),
        name="hidden_terms",
    )(index, *gathered, down_t)


def on_device(
    key_grad, value_grad, rope_grad, key_lift, value_lift, latent, norm_gain, doc_lengths, hidden, down_proj
):
    heads, groups = 4, 8
    core_bit, x_bit, y_bit = 1, 2, 4
    share = key_grad.shape[0] // heads
    kva = down_proj.shape[1]
    block = kva // groups
    half = (kva - latent.shape[1]) // 2

    def swap_head(array, bits):
        return lax.ppermute(array, "head", [(i, i ^ bits) for i in range(heads)])

    def swap_group(array, bits_of):
        return lax.ppermute(array, "group", [(i, i ^ bits_of(i)) for i in range(groups)])

    def first_bit(i):
        return y_bit if i & core_bit else x_bit

    def second_bit(i):
        return x_bit if i & core_bit else y_bit

    me, mine = lax.axis_index("head"), lax.axis_index("group")
    other = mine ^ core_bit
    first = jnp.where(mine & core_bit == 0, x_bit, y_bit)
    second = first ^ (x_bit | y_bit)
    both = x_bit | y_bit
    index = jnp.stack(
        [me, me ^ 1, me ^ 2, me ^ 3]
        + [mine ^ both, mine ^ first, mine ^ second, mine]
        + [other ^ both, other ^ second, other ^ first, other]
    ).astype(jnp.int32)

    freq = 10000.0 ** (-(2.0 * np.arange(half)) / (2.0 * half))
    freq = jnp.asarray(np.broadcast_to(freq[:, None], (half, share)), F32)
    gain = norm_gain.reshape(1, -1)
    sibling_hidden = swap_group(hidden, lambda i: core_bit)

    def terms(which, dtype):
        return partial_terms(
            which, dtype, index, doc_lengths, key_grad, value_grad, rope_grad, key_lift, value_lift,
            latent, gain, freq, share, block,
        )

    p3, p1 = terms((3, 1), BF16)
    got3 = swap_head(p3, 1)
    got1 = swap_head(p1, 1)
    p2, p0 = terms((2, 0), F32)
    pair2 = (p2 + got3.astype(F32)).astype(BF16)
    got2 = swap_head(pair2, 2)
    q0 = (p0 + got1.astype(F32) + got2.astype(F32)).astype(BF16)
    q2 = swap_head(q0, 2)
    q1 = swap_head(q0, 1)
    q3 = swap_head(q2, 1)
    gathered = (q0, q1, q2, q3)
    sibling = tuple(swap_group(q, lambda i: core_bit) for q in gathered)

    send, keep = weight_terms(index, gathered, sibling, hidden, sibling_hidden)
    got = swap_group(send, first_bit)
    hidden_grad = hidden_terms(index, gathered, down_proj.T, block)
    summed = keep + got.astype(F32)
    last = swap_group(summed[:block].astype(BF16), second_bit)
    weight_grad = summed[block:] + last.astype(F32)
    return (hidden_grad, weight_grad)


def solution(mesh):
    shape = dict(mesh.shape)
    paired = shape["head"] == 4 and shape["group"] == 8
    return jax.shard_map(
        on_device if paired else on_device_any,
        mesh=mesh,
        in_specs=(
            P("group", "head"),
            P("group", "head"),
            P("group", "head"),
            P(None, "head"),
            P(None, "head"),
            P("group", None),
            P(),
            P("group", None),
            P("group", "head"),
            P("head", None),
        ),
        out_specs=(P("group", "head"), P("group", "head")),
        check_vma=False,
    )
```

```python
import functools
import math

import jax
import jax.numpy as jnp
from jax import lax
from jax.experimental import pallas as pl
from jax.experimental.pallas import tpu as pltpu
from jax.sharding import PartitionSpec as P

F32 = jnp.float32
BF16 = jnp.bfloat16
LAST = (((1,), (1,)), ((), ()))
FIRST = (((0,), (0,)), ((), ()))
MIB = 1 << 20


def positions(lengths, token_index):
    doc_ends = jnp.cumsum(lengths, axis=1)
    doc_start = jnp.max(jnp.where(doc_ends <= token_index[:, None], doc_ends, 0), axis=1)
    return token_index - doc_start


def kva_rows_grad(stacked, latent, norm_gain, position):
    width = latent.shape[1]
    latent_part = stacked[:, :width]
    rotary_part = stacked[:, width:]
    values = latent.astype(F32)
    inverse_rms = lax.rsqrt(jnp.mean(values * values, axis=1, keepdims=True) + 1e-06)
    scaled_grad = latent_part * norm_gain[None, :]
    norm_grad = inverse_rms * (
        scaled_grad
        - values * inverse_rms * inverse_rms * jnp.mean(scaled_grad * values, axis=1, keepdims=True)
    )
    half_width = rotary_part.shape[1] // 2
    inv_freq = 10000.0 ** (-(2.0 * jnp.arange(half_width, dtype=F32)) / (2.0 * half_width))
    angles = position.astype(F32)[:, None] * inv_freq[None, :]
    cosine = jnp.cos(angles)
    sine = jnp.sin(angles)
    first_half = rotary_part[:, :half_width]
    second_half = rotary_part[:, half_width:]
    rot_first = first_half * cosine + second_half * sine
    rot_second = second_half * cosine - first_half * sine
    return jnp.concatenate([norm_grad, rot_first, rot_second], axis=1).astype(BF16)


def on_device_any(
    key_grad, value_grad, rope_grad, key_lift, value_lift, latent, norm_gain, doc_lengths, hidden, down_proj
):
    seq_len = key_grad.shape[0]
    rope = down_proj.shape[1] - latent.shape[1]
    head_terms = lax.dot_general(key_grad, key_lift, LAST, preferred_element_type=F32)
    head_terms = head_terms + lax.dot_general(value_grad, value_lift, LAST, preferred_element_type=F32)
    heads_here = rope_grad.shape[1] // rope
    rope_terms = jnp.sum(rope_grad.reshape(seq_len, heads_here, rope), axis=1, dtype=F32)
    stacked = jnp.concatenate([head_terms, rope_terms], axis=1)
    shared = lax.psum_scatter(stacked, "head", scatter_dimension=0, tiled=True)
    share_rows = shared.shape[0]
    first_row = lax.axis_index("head") * share_rows
    own_latent = lax.dynamic_slice_in_dim(latent, first_row, share_rows, 0)
    token_index = first_row + jnp.arange(share_rows, dtype=jnp.int32)
    row_lengths = jnp.broadcast_to(doc_lengths, (share_rows, doc_lengths.shape[1]))
    own_grad = kva_rows_grad(shared, own_latent, norm_gain, positions(row_lengths, token_index))
    kva_grad = lax.all_gather(own_grad, "head", axis=0, tiled=True)
    hidden_grad = lax.dot_general(kva_grad, down_proj, LAST, preferred_element_type=F32).astype(BF16)
    weight_grad = lax.psum_scatter(
        lax.dot_general(kva_grad, hidden, FIRST, preferred_element_type=F32),
        "group",
        scatter_dimension=0,
        tiled=True,
    )
    return (hidden_grad, weight_grad)


def axis_bits():
    return 1, 2, 4


def row_order(blocks):
    core, x, y = axis_bits()
    mine = lax.axis_index("group")
    first = jnp.where(mine & core == 0, x, y)
    other, second, both = mine ^ core, first ^ (x | y), x | y
    order = [mine ^ both, mine ^ first, mine ^ second, mine]
    order += [other ^ both, other ^ second, other ^ first, other]
    assert len(order) == blocks
    return order


def partial_kernel(
    lengths, kg, vg, rg, kl, vl, lat, gain,
    out_a, out_b, kg_v, vg_v, rg_v, kl_v, vl_v, lat_v, gain_v, lengths_s, sems, acc, rope_acc, values, turns, rows,
    *, which, block, chunks,
):
    share = out_a.shape[1]
    latent, rope = acc.shape[0], rope_acc.shape[0]
    half = rope // 2
    shares = [lax.axis_index("head") ^ r for r in which]
    places = [pl.ds(pl.multiple_of(r * share, share), share) for r in shares]
    sides = [slice(side * share, (side + 1) * share) for side in range(2)]

    def columns(ref, chunk):
        width = ref.shape[1] // chunks
        return slice(chunk * width, (chunk + 1) * width)

    def copies_of(chunk):
        pairs = [
            (src.at[:, columns(src, chunk)], dst.at[:, columns(src, chunk)])
            for src, dst in ((kl, kl_v), (vl, vl_v))
        ]
        for src, dst in ((kg, kg_v), (vg, vg_v), (rg, rg_v)):
            for place, side in zip(places, sides):
                pairs.append((src.at[place, columns(src, chunk)], dst.at[side, columns(src, chunk)]))
        return [pltpu.make_async_copy(src, dst, sems.at[chunk, i]) for i, (src, dst) in enumerate(pairs)]

    small_copies = [
        pltpu.make_async_copy(lat.at[place, :], lat_v.at[side, :], sems.at[chunks, i])
        for i, (place, side) in enumerate(zip(places, sides))
    ]
    small_copies.append(pltpu.make_async_copy(gain, gain_v, sems.at[chunks, 2]))
    small_copies.append(pltpu.make_async_copy(lengths, lengths_s, sems.at[chunks, 3]))
    all_copies = [copies_of(chunk) for chunk in range(chunks)]
    for copy in all_copies[0] + small_copies + [copy for copies in all_copies[1:] for copy in copies]:
        copy.start()

    fold_shape = (rope, rg.shape[1] // chunks)
    fold = lax.rem(lax.broadcasted_iota(jnp.int32, fold_shape, 1), rope) == lax.broadcasted_iota(
        jnp.int32, fold_shape, 0
    )
    fold = fold.astype(BF16)

    for chunk in range(chunks):
        for copy in all_copies[chunk]:
            copy.wait()
        here = columns(kg, chunk)
        term = lax.dot_general(kl_v[:, here], kg_v[:, here], LAST, preferred_element_type=F32)
        term += lax.dot_general(vl_v[:, here], vg_v[:, here], LAST, preferred_element_type=F32)
        rope_term = lax.dot_general(fold, rg_v[:, columns(rg, chunk)], LAST, preferred_element_type=F32)
        acc[...] = term if chunk == 0 else acc[...] + term
        rope_acc[...] = rope_term if chunk == 0 else rope_acc[...] + rope_term
        if chunk == 0:
            for copy in small_copies:
                copy.wait()
            values[...] = lat_v[...].astype(F32).T
            lane = lax.broadcasted_iota(jnp.int32, (1, share), 1)
            pair = lax.broadcasted_iota(jnp.int32, (half, share), 0).astype(F32)
            freq = jnp.exp(pair * (-math.log(10000.0) / half))
            for r, side in zip(shares, sides):
                token = r * share + lane
                start = jnp.zeros_like(token)
                end = jnp.int32(0)
                for doc in range(lengths.shape[1]):
                    end = end + lengths_s[0, doc]
                    start = jnp.maximum(start, jnp.where(end <= token, end, 0))
                angle = (token - start).astype(F32) * freq
                turns[:half, side] = jnp.cos(angle)
                turns[half:, side] = jnp.sin(angle)

    gains = jnp.broadcast_to(gain_v[...], (share, latent)).T
    gains = jnp.concatenate([gains, gains], axis=1)
    c = values[...]
    inv = lax.rsqrt(jnp.mean(c * c, axis=0, keepdims=True) + 1e-06)
    g = acc[...] * gains
    mean = jnp.mean(g * c, axis=0, keepdims=True)
    rows[:latent, :] = inv * (g - c * (inv * inv * mean))
    first, second = rope_acc[:half, :], rope_acc[half:, :]
    rows[latent : latent + half, :] = first * turns[:half, :] + second * turns[half:, :]
    rows[latent + half :, :] = second * turns[:half, :] - first * turns[half:, :]
    ordered = jnp.concatenate(
        [rows[pl.ds(pl.multiple_of(r * block, 8), block), :] for r in row_order(rows.shape[0] // block)], axis=0
    )
    out_a[...] = ordered[:, :share].astype(out_a.dtype)
    out_b[...] = ordered[:, share:].astype(out_b.dtype)


def partial_terms(which, out_dtype, doc_lengths, kg, vg, rg, kl, vl, latent, gain, share, rope, block):
    key_cols = kg.shape[1]
    width = latent.shape[1]
    kva = width + rope
    chunks = 8 if key_cols % 1024 == 0 and rg.shape[1] % 1024 == 0 else 1
    operands = [
        pltpu.with_memory_space_constraint(x, pltpu.HBM) for x in (doc_lengths, kg, vg, rg, kl, vl, latent, gain)
    ]
    return pl.pallas_call(
        functools.partial(partial_kernel, which=which, block=block, chunks=chunks),
        in_specs=[pl.BlockSpec(memory_space=pltpu.HBM)] * len(operands),
        out_specs=[pl.BlockSpec(memory_space=pltpu.VMEM)] * 2,
        scratch_shapes=[
            pltpu.VMEM((2 * share, key_cols), BF16),
            pltpu.VMEM((2 * share, key_cols), BF16),
            pltpu.VMEM((2 * share, rg.shape[1]), BF16),
            pltpu.VMEM((width, key_cols), BF16),
            pltpu.VMEM((width, key_cols), BF16),
            pltpu.VMEM((2 * share, width), BF16),
            pltpu.VMEM(gain.shape, F32),
            pltpu.SMEM(doc_lengths.shape, jnp.int32),
            pltpu.SemaphoreType.DMA((chunks + 1, 8)),
            pltpu.VMEM((width, 2 * share), F32),
            pltpu.VMEM((rope, 2 * share), F32),
            pltpu.VMEM((width, 2 * share), F32),
            pltpu.VMEM((rope, 2 * share), F32),
            pltpu.VMEM((kva, 2 * share), F32),
        ],
        out_shape=[pltpu.VMEM((kva, share), out_dtype)] * 2,
        compiler_params=pltpu.CompilerParams(vmem_limit_bytes=28 * MIB),
        cost_estimate=pl.CostEstimate(
            flops=2 * 2 * share * width * key_cols * 2,
            bytes_accessed=2 * (2 * width * key_cols + 2 * share * (2 * key_cols + rg.shape[1])),
            transcendentals=0,
        ),
        name="partial_terms",
    )(*operands)


def weight_kernel(*refs):
    own, sibling = refs[:4], refs[4:8]
    hidden, sibling_hidden, send, keep = refs[8:12]
    half, share = own[0].shape[0] // 2, own[0].shape[1]
    columns = hidden.shape[1]
    width = 256 if columns % 256 == 0 else columns
    left = jnp.concatenate([r[:half] for r in own] + [r[half:] for r in sibling], axis=1)
    me = lax.axis_index("head")
    places = [pl.ds(pl.multiple_of((me ^ r) * share, share), share) for r in range(4)]
    for n in range(columns // width):
        cols = slice(n * width, (n + 1) * width)
        right = [ref[place, cols] for ref in (hidden, sibling_hidden) for place in places]
        result = jnp.dot(left, jnp.concatenate(right, axis=0), preferred_element_type=F32)
        send[:, cols] = result[: half // 2].astype(send.dtype)
        keep[:, cols] = result[half // 2 :]


def weight_terms(own, sibling, hidden, sibling_hidden):
    kva, share = own[0].shape
    columns = hidden.shape[1]
    quarter = kva // 4
    vmem = pl.BlockSpec(memory_space=pltpu.VMEM)
    return pl.pallas_call(
        weight_kernel,
        in_specs=[vmem] * 10,
        out_specs=[vmem] * 2,
        out_shape=[
            jax.ShapeDtypeStruct((quarter, columns), BF16),
            jax.ShapeDtypeStruct((quarter, columns), F32),
        ],
        compiler_params=pltpu.CompilerParams(vmem_limit_bytes=32 * MIB),
        cost_estimate=pl.CostEstimate(
            flops=2 * (kva // 2) * 8 * share * columns, bytes_accessed=8 * MIB, transcendentals=0
        ),
        name="weight_terms",
    )(*own, *sibling, hidden, sibling_hidden)


def hidden_kernel(q0, q1, q2, q3, down_t, out, kva, natural, *, block):
    share = q0.shape[1]

    @pl.when(pl.program_id(0) == 0)
    def _():
        me = lax.axis_index("head")
        order = row_order(q0.shape[0] // block)
        for r, q in enumerate((q0, q1, q2, q3)):
            ordered = q[...].astype(F32)
            for i, place in enumerate(order):
                natural[pl.ds(pl.multiple_of(place * block, 8), block), :] = ordered[i * block : (i + 1) * block]
            kva[pl.ds(pl.multiple_of((me ^ r) * share, share), share), :] = natural[...].T.astype(BF16)

    out[...] = jnp.dot(kva[...], down_t[...], preferred_element_type=F32).astype(out.dtype)


def hidden_terms(gathered, down_t, block):
    kva, share = gathered[0].shape
    columns = down_t.shape[1]
    col_block = columns // 2 if columns % 256 == 0 else columns
    tokens = 4 * share
    whole = pl.BlockSpec((kva, share), lambda n: (0, 0))
    return pl.pallas_call(
        functools.partial(hidden_kernel, block=block),
        grid=(columns // col_block,),
        in_specs=[whole] * 4 + [pl.BlockSpec((kva, col_block), lambda n: (0, n))],
        out_specs=pl.BlockSpec((tokens, col_block), lambda n: (0, n)),
        scratch_shapes=[pltpu.VMEM((tokens, kva), BF16), pltpu.VMEM((kva, share), F32)],
        out_shape=jax.ShapeDtypeStruct((tokens, columns), BF16),
        compiler_params=pltpu.CompilerParams(vmem_limit_bytes=32 * MIB),
        cost_estimate=pl.CostEstimate(
            flops=2 * tokens * kva * columns, bytes_accessed=5 * MIB, transcendentals=0
        ),
        name="hidden_terms",
    )(*gathered, down_t)


def on_device(
    key_grad, value_grad, rope_grad, key_lift, value_lift, latent, norm_gain, doc_lengths, hidden, down_proj
):
    heads, groups = 4, 8
    core_bit, x_bit, y_bit = axis_bits()
    share = key_grad.shape[0] // heads
    kva = down_proj.shape[1]
    block = kva // groups

    def swap_head(array, bits):
        return lax.ppermute(array, "head", [(i, i ^ bits) for i in range(heads)])

    def swap_group(array, bits_of):
        return lax.ppermute(array, "group", [(i, i ^ bits_of(i)) for i in range(groups)])

    def first_bit(i):
        return y_bit if i & core_bit else x_bit

    def second_bit(i):
        return x_bit if i & core_bit else y_bit

    gain = norm_gain.reshape(1, -1)
    sibling_hidden = swap_group(hidden, lambda i: core_bit)

    def terms(which, dtype):
        return partial_terms(
            which, dtype, doc_lengths, key_grad, value_grad, rope_grad, key_lift, value_lift,
            latent, gain, share, kva - latent.shape[1], block,
        )

    p3, p1 = terms((3, 1), BF16)
    got3 = swap_head(p3, 1)
    got1 = swap_head(p1, 1)
    p2, p0 = terms((2, 0), F32)
    pair2 = (p2 + got3.astype(F32)).astype(BF16)
    got2 = swap_head(pair2, 2)
    q0 = (p0 + got1.astype(F32) + got2.astype(F32)).astype(BF16)
    q2 = swap_head(q0, 2)
    q1 = swap_head(q0, 1)
    q3 = swap_head(q2, 1)
    gathered = (q0, q1, q2, q3)
    sibling = tuple(swap_group(q, lambda i: core_bit) for q in gathered)

    send, keep = weight_terms(gathered, sibling, hidden, sibling_hidden)
    got = swap_group(send, first_bit)
    hidden_grad = hidden_terms(gathered, down_proj.T, block)
    summed = keep + got.astype(F32)
    last = swap_group(summed[:block].astype(BF16), second_bit)
    weight_grad = summed[block:] + last.astype(F32)
    return (hidden_grad, weight_grad)


def solution(mesh):
    shape = dict(mesh.shape)
    paired = shape["head"] == 4 and shape["group"] == 8
    return jax.shard_map(
        on_device if paired else on_device_any,
        mesh=mesh,
        in_specs=(
            P("group", "head"),
            P("group", "head"),
            P("group", "head"),
            P(None, "head"),
            P(None, "head"),
            P("group", None),
            P(),
            P("group", None),
            P("group", "head"),
            P("head", None),
        ),
        out_specs=(P("group", "head"), P("group", "head")),
        check_vma=False,
    )
```

```python
import functools
import math

import jax
import jax.numpy as jnp
from jax import lax
from jax.experimental import pallas as pl
from jax.experimental.pallas import tpu as pltpu
from jax.sharding import PartitionSpec as P

F32 = jnp.float32
BF16 = jnp.bfloat16
LAST = (((1,), (1,)), ((), ()))
FIRST = (((0,), (0,)), ((), ()))
MIB = 1 << 20


def positions(lengths, token_index):
    doc_ends = jnp.cumsum(lengths, axis=1)
    doc_start = jnp.max(jnp.where(doc_ends <= token_index[:, None], doc_ends, 0), axis=1)
    return token_index - doc_start


def kva_rows_grad(stacked, latent, norm_gain, position):
    width = latent.shape[1]
    latent_part = stacked[:, :width]
    rotary_part = stacked[:, width:]
    values = latent.astype(F32)
    inverse_rms = lax.rsqrt(jnp.mean(values * values, axis=1, keepdims=True) + 1e-06)
    scaled_grad = latent_part * norm_gain[None, :]
    norm_grad = inverse_rms * (
        scaled_grad
        - values * inverse_rms * inverse_rms * jnp.mean(scaled_grad * values, axis=1, keepdims=True)
    )
    half_width = rotary_part.shape[1] // 2
    inv_freq = 10000.0 ** (-(2.0 * jnp.arange(half_width, dtype=F32)) / (2.0 * half_width))
    angles = position.astype(F32)[:, None] * inv_freq[None, :]
    cosine = jnp.cos(angles)
    sine = jnp.sin(angles)
    first_half = rotary_part[:, :half_width]
    second_half = rotary_part[:, half_width:]
    rot_first = first_half * cosine + second_half * sine
    rot_second = second_half * cosine - first_half * sine
    return jnp.concatenate([norm_grad, rot_first, rot_second], axis=1).astype(BF16)


def on_device_any(
    key_grad, value_grad, rope_grad, key_lift, value_lift, latent, norm_gain, doc_lengths, hidden, down_proj
):
    seq_len = key_grad.shape[0]
    rope = down_proj.shape[1] - latent.shape[1]
    head_terms = lax.dot_general(key_grad, key_lift, LAST, preferred_element_type=F32)
    head_terms = head_terms + lax.dot_general(value_grad, value_lift, LAST, preferred_element_type=F32)
    heads_here = rope_grad.shape[1] // rope
    rope_terms = jnp.sum(rope_grad.reshape(seq_len, heads_here, rope), axis=1, dtype=F32)
    stacked = jnp.concatenate([head_terms, rope_terms], axis=1)
    shared = lax.psum_scatter(stacked, "head", scatter_dimension=0, tiled=True)
    share_rows = shared.shape[0]
    first_row = lax.axis_index("head") * share_rows
    own_latent = lax.dynamic_slice_in_dim(latent, first_row, share_rows, 0)
    token_index = first_row + jnp.arange(share_rows, dtype=jnp.int32)
    row_lengths = jnp.broadcast_to(doc_lengths, (share_rows, doc_lengths.shape[1]))
    own_grad = kva_rows_grad(shared, own_latent, norm_gain, positions(row_lengths, token_index))
    kva_grad = lax.all_gather(own_grad, "head", axis=0, tiled=True)
    hidden_grad = lax.dot_general(kva_grad, down_proj, LAST, preferred_element_type=F32).astype(BF16)
    weight_grad = lax.psum_scatter(
        lax.dot_general(kva_grad, hidden, FIRST, preferred_element_type=F32),
        "group",
        scatter_dimension=0,
        tiled=True,
    )
    return (hidden_grad, weight_grad)


def axis_bits():
    return 1, 2, 4


def row_order(blocks):
    core, x, y = axis_bits()
    mine = lax.axis_index("group")
    first = jnp.where(mine & core == 0, x, y)
    other, second, both = mine ^ core, first ^ (x | y), x | y
    order = [mine ^ both, mine ^ first, other ^ both, other ^ second]
    order += [mine ^ second, mine, other ^ first, other]
    assert len(order) == blocks
    return order


def partial_kernel(*refs, which, dtypes, rope, block, chunks, lifts_here):
    count = len(which)
    lengths, kg, vg, rg, kl, vl, lat, gain = refs[:8]
    outs, refs = refs[8 : 8 + count], refs[8 + count :]
    if lifts_here:
        kl_v, vl_v = kl, vl
    else:
        (kl_v, vl_v), refs = refs[:2], refs[2:]
    kg_v, vg_v, rg_v, lat_v, gain_v, lengths_s, sems, acc, rope_acc, values, turns, rows = refs
    share = outs[0].shape[1]
    latent = lat.shape[1]
    half = rope // 2
    shares = [lax.axis_index("head") ^ r for r in which]
    places = [pl.ds(pl.multiple_of(r * share, share), share) for r in shares]
    sides = [slice(side * share, (side + 1) * share) for side in range(count)]

    def columns(ref, chunk):
        width = ref.shape[1] // chunks
        return slice(chunk * width, (chunk + 1) * width)

    def copies_of(chunk):
        pairs = []
        if not lifts_here:
            for src, dst in ((kl, kl_v), (vl, vl_v)):
                pairs.append((src.at[:, columns(src, chunk)], dst.at[:, columns(src, chunk)]))
        for src, dst in ((kg, kg_v), (vg, vg_v), (rg, rg_v)):
            for place, side in zip(places, sides):
                pairs.append((src.at[place, columns(src, chunk)], dst.at[side, columns(src, chunk)]))
        return [pltpu.make_async_copy(src, dst, sems.at[chunk, i]) for i, (src, dst) in enumerate(pairs)]

    small = [(lat.at[place, :], lat_v.at[side, :]) for place, side in zip(places, sides)]
    small += [(gain, gain_v), (lengths, lengths_s)]
    small_copies = [pltpu.make_async_copy(src, dst, sems.at[chunks, i]) for i, (src, dst) in enumerate(small)]
    all_copies = [copies_of(chunk) for chunk in range(chunks)]
    for copy in all_copies[0] + small_copies + [copy for copies in all_copies[1:] for copy in copies]:
        copy.start()

    fold_shape = (rope, rg.shape[1] // chunks)
    fold = lax.rem(lax.broadcasted_iota(jnp.int32, fold_shape, 1), rope) == lax.broadcasted_iota(
        jnp.int32, fold_shape, 0
    )
    fold = fold.astype(BF16)

    for chunk in range(chunks):
        for copy in all_copies[chunk]:
            copy.wait()
        here = columns(kg, chunk)
        term = lax.dot_general(kg_v[:, here], kl_v[:, here], LAST, preferred_element_type=F32)
        term += lax.dot_general(vg_v[:, here], vl_v[:, here], LAST, preferred_element_type=F32)
        rope_term = lax.dot_general(fold, rg_v[:, columns(rg, chunk)], LAST, preferred_element_type=F32)
        acc[...] = term if chunk == 0 else acc[...] + term
        rope_acc[...] = rope_term if chunk == 0 else rope_acc[...] + rope_term
        if chunk == 0:
            for copy in small_copies:
                copy.wait()
            values[...] = lat_v[...].astype(F32).T
            lane = lax.broadcasted_iota(jnp.int32, (1, share), 1)
            pair = lax.broadcasted_iota(jnp.int32, (half, share), 0).astype(F32)
            freq = jnp.exp(pair * (-math.log(10000.0) / half))
            for r, side in zip(shares, sides):
                token = r * share + lane
                start = jnp.zeros_like(token)
                end = jnp.int32(0)
                for doc in range(lengths.shape[1]):
                    end = end + lengths_s[0, doc]
                    start = jnp.maximum(start, jnp.where(end <= token, end, 0))
                angle = (token - start).astype(F32) * freq
                turns[:half, side] = jnp.cos(angle)
                turns[half:, side] = jnp.sin(angle)

    gains = jnp.broadcast_to(gain_v[...], (share, latent)).T
    gains = jnp.concatenate([gains] * count, axis=1)
    c = values[...]
    inv = lax.rsqrt(jnp.mean(c * c, axis=0, keepdims=True) + 1e-06)
    g = acc[...].T * gains
    mean = jnp.mean(g * c, axis=0, keepdims=True)
    rows[:latent, :] = inv * (g - c * (inv * inv * mean))
    first, second = rope_acc[:half, :], rope_acc[half:, :]
    rows[latent : latent + half, :] = first * turns[:half, :] + second * turns[half:, :]
    rows[latent + half :, :] = second * turns[:half, :] - first * turns[half:, :]
    ordered = jnp.concatenate(
        [rows[pl.ds(pl.multiple_of(r * block, 8), block), :] for r in row_order(rows.shape[0] // block)], axis=0
    )
    for out, dtype, side in zip(outs, dtypes, sides):
        out[...] = ordered[:, side].astype(dtype)


def partial_terms(which, dtypes, doc_lengths, kg, vg, rg, kl, vl, latent, gain, share, rope, block, lifts_here):
    key_cols = kg.shape[1]
    width = latent.shape[1]
    kva = width + rope
    tokens = len(which) * share
    chunks = 4 if lifts_here else 8
    if key_cols % (chunks * 128) or rg.shape[1] % (chunks * 128):
        chunks = 1
    operands = (doc_lengths, kg, vg, rg, kl, vl, latent, gain)
    spaces = [pltpu.VMEM if lifts_here and i in (4, 5) else pltpu.HBM for i in range(len(operands))]
    out_shape = [pltpu.VMEM((kva, share), dtype) for dtype in dtypes]
    if not lifts_here:
        out_shape += [pltpu.VMEM(kl.shape, BF16), pltpu.VMEM(vl.shape, BF16)]
    return pl.pallas_call(
        functools.partial(
            partial_kernel, which=which, dtypes=dtypes, rope=rope, block=block, chunks=chunks, lifts_here=lifts_here
        ),
        in_specs=[pl.BlockSpec(memory_space=space) for space in spaces],
        out_specs=[pl.BlockSpec(memory_space=pltpu.VMEM)] * len(out_shape),
        scratch_shapes=[
            pltpu.VMEM((tokens, key_cols), BF16),
            pltpu.VMEM((tokens, key_cols), BF16),
            pltpu.VMEM((tokens, rg.shape[1]), BF16),
            pltpu.VMEM((tokens, width), BF16),
            pltpu.VMEM(gain.shape, F32),
            pltpu.SMEM(doc_lengths.shape, jnp.int32),
            pltpu.SemaphoreType.DMA((chunks + 1, 2 + 3 * len(which))),
            pltpu.VMEM((tokens, width), F32),
            pltpu.VMEM((rope, tokens), F32),
            pltpu.VMEM((width, tokens), F32),
            pltpu.VMEM((rope, tokens), F32),
            pltpu.VMEM((kva, tokens), F32),
        ],
        out_shape=out_shape,
        compiler_params=pltpu.CompilerParams(vmem_limit_bytes=28 * MIB),
        cost_estimate=pl.CostEstimate(
            flops=2 * tokens * width * key_cols * 2,
            bytes_accessed=2 * (2 * width * key_cols + tokens * (2 * key_cols + rg.shape[1])),
            transcendentals=0,
        ),
        name="partial_terms",
    )(*[pltpu.with_memory_space_constraint(x, space) for x, space in zip(operands, spaces)])


def weight_kernel(*refs, part, parts):
    own, sibling = refs[:4], refs[4:8]
    hidden, sibling_hidden = refs[8:10]
    outs = refs[10:]
    share = own[0].shape[1]
    block = outs[0].shape[0]
    count = len(outs) * block

    def rows_of(ref, side):
        skip = 2 * part * count if ref.shape[0] == 2 * parts * count else 0
        return ref[skip + side * count : skip + (side + 1) * count]

    left = jnp.concatenate([rows_of(r, 0) for r in own] + [rows_of(r, 1) for r in sibling], axis=1)
    columns = hidden.shape[1]
    width = 256 if columns % 256 == 0 else columns
    me = lax.axis_index("head")
    places = [pl.ds(pl.multiple_of((me ^ r) * share, share), share) for r in range(4)]
    for n in range(columns // width):
        cols = slice(n * width, (n + 1) * width)
        right = [ref[place, cols] for ref in (hidden, sibling_hidden) for place in places]
        result = jnp.dot(left, jnp.concatenate(right, axis=0), preferred_element_type=F32)
        for i, out in enumerate(outs):
            out[:, cols] = result[i * block : (i + 1) * block].astype(out.dtype)


def weight_terms(own, sibling, hidden, sibling_hidden, block, part, parts, dtypes):
    columns = hidden.shape[1]
    vmem = pl.BlockSpec(memory_space=pltpu.VMEM)
    operands = (*own, *sibling, hidden, sibling_hidden)
    return pl.pallas_call(
        functools.partial(weight_kernel, part=part, parts=parts),
        in_specs=[vmem] * len(operands),
        out_specs=[vmem] * len(dtypes),
        out_shape=[pltpu.VMEM((block, columns), dtype) for dtype in dtypes],
        compiler_params=pltpu.CompilerParams(vmem_limit_bytes=24 * MIB),
        cost_estimate=pl.CostEstimate(flops=1000, bytes_accessed=1000, transcendentals=0),
        name="weight_terms",
    )(*[pltpu.with_memory_space_constraint(x, pltpu.VMEM) for x in operands])


def natural_kernel(*refs, block):
    shares, out, natural = refs[:-2], refs[-2], refs[-1]
    me = lax.axis_index("head")
    order = row_order(natural.shape[0] // block)
    share = shares[0].shape[1]
    for r, q in enumerate(shares):
        ordered = q[...].astype(F32)
        for i, place in enumerate(order):
            natural[pl.ds(pl.multiple_of(place * block, 8), block), :] = ordered[i * block : (i + 1) * block]
        out[pl.ds(pl.multiple_of((me ^ r) * share, share), share), :] = natural[...].T.astype(BF16)


def natural_rows(gathered, block):
    kva, share = gathered[0].shape
    return pl.pallas_call(
        functools.partial(natural_kernel, block=block),
        in_specs=[pl.BlockSpec(memory_space=pltpu.VMEM)] * len(gathered),
        out_specs=pl.BlockSpec(memory_space=pltpu.VMEM),
        scratch_shapes=[pltpu.VMEM((kva, share), F32)],
        out_shape=pltpu.VMEM((len(gathered) * share, kva), BF16),
        compiler_params=pltpu.CompilerParams(vmem_limit_bytes=24 * MIB),
        cost_estimate=pl.CostEstimate(flops=1000, bytes_accessed=1000, transcendentals=0),
        name="natural_rows",
    )(*[pltpu.with_memory_space_constraint(x, pltpu.VMEM) for x in gathered])


def hidden_kernel(rows, down_t, out):
    out[...] = jnp.dot(rows[...], down_t[...], preferred_element_type=F32).astype(out.dtype)


def hidden_terms(rows, down_t):
    tokens = rows.shape[0]
    kva, columns = down_t.shape
    col_block = columns // 2 if columns % 256 == 0 else columns
    return pl.pallas_call(
        hidden_kernel,
        grid=(columns // col_block,),
        in_specs=[pl.BlockSpec((tokens, kva), lambda n: (0, 0)), pl.BlockSpec((kva, col_block), lambda n: (0, n))],
        out_specs=pl.BlockSpec((tokens, col_block), lambda n: (0, n)),
        out_shape=jax.ShapeDtypeStruct((tokens, columns), BF16),
        compiler_params=pltpu.CompilerParams(vmem_limit_bytes=24 * MIB),
        cost_estimate=pl.CostEstimate(flops=1000, bytes_accessed=1000, transcendentals=0),
        name="hidden_terms",
    )(rows, down_t)


def on_device(
    key_grad, value_grad, rope_grad, key_lift, value_lift, latent, norm_gain, doc_lengths, hidden, down_proj
):
    heads, groups = 4, 8
    core_bit, x_bit, y_bit = axis_bits()
    share = key_grad.shape[0] // heads
    kva = down_proj.shape[1]
    block = kva // groups

    def swap_head(array, bits):
        return lax.ppermute(array, "head", [(i, i ^ bits) for i in range(heads)])

    def swap_group(array, bits_of):
        return lax.ppermute(array, "group", [(i, i ^ bits_of(i)) for i in range(groups)])

    def first_bit(i):
        return y_bit if i & core_bit else x_bit

    def second_bit(i):
        return x_bit if i & core_bit else y_bit

    gain = norm_gain.reshape(1, -1)
    def terms(which, dtypes, lifts, lifts_here):
        return partial_terms(
            which, dtypes, doc_lengths, key_grad, value_grad, rope_grad, *lifts,
            latent, gain, share, kva - latent.shape[1], block, lifts_here,
        )

    p3, *lifts = terms((3,), (BF16,), (key_lift, value_lift), False)
    got3 = swap_head(p3, 1)
    p2, p1 = terms((2, 1), (F32, BF16), lifts, True)
    pair2 = (p2 + got3.astype(F32)).astype(BF16)
    pair2, p1, hidden, *lifts = lax.optimization_barrier((pair2, p1, hidden, *lifts))
    got2 = swap_head(pair2, 2)
    got1 = swap_head(p1, 1)
    sibling_hidden = swap_group(hidden, lambda i: core_bit)
    (p0,) = terms((0,), (F32,), lifts, True)
    q0 = (p0 + got1.astype(F32) + got2.astype(F32)).astype(BF16)
    q2 = swap_head(q0, 2)
    q1 = swap_head(q0, 1)
    q3 = swap_head(q2, 1)
    gathered = (q0, q1, q2, q3)
    sibling = tuple(swap_group(q, lambda i: core_bit) for q in gathered)

    def weights(part, dtypes):
        return weight_terms(gathered, sibling, hidden, sibling_hidden, block, part, 2, dtypes)

    for_both, for_first = weights(0, (BF16, BF16))
    got_both = swap_group(for_both, first_bit)
    sibling_hidden, for_first, for_both = lax.optimization_barrier((sibling_hidden, for_first, for_both))
    for_second, mine = weights(1, (F32, F32))
    kva_rows = natural_rows(gathered, block)
    for_first, for_second, kva_rows = lax.optimization_barrier((for_first, for_second, kva_rows))
    got_first = swap_group(for_first, first_bit)
    hidden_grad = hidden_terms(kva_rows, down_proj.T)
    got_second = swap_group((for_second + got_both.astype(F32)).astype(BF16), second_bit)
    weight_grad = mine + got_first.astype(F32) + got_second.astype(F32)
    return (hidden_grad, weight_grad)


def solution(mesh):
    shape = dict(mesh.shape)
    paired = shape["head"] == 4 and shape["group"] == 8
    return jax.shard_map(
        on_device if paired else on_device_any,
        mesh=mesh,
        in_specs=(
            P("group", "head"),
            P("group", "head"),
            P("group", "head"),
            P(None, "head"),
            P(None, "head"),
            P("group", None),
            P(),
            P("group", None),
            P("group", "head"),
            P("head", None),
        ),
        out_specs=(P("group", "head"), P("group", "head")),
        check_vma=False,
    )
```

```python
import functools
import math

import jax
import jax.numpy as jnp
from jax import lax
from jax.experimental import pallas as pl
from jax.experimental.pallas import tpu as pltpu
from jax.sharding import PartitionSpec as P

F32 = jnp.float32
BF16 = jnp.bfloat16
LAST = (((1,), (1,)), ((), ()))
FIRST = (((0,), (0,)), ((), ()))
MIB = 1 << 20
SHORT = pl.CostEstimate(flops=1000, bytes_accessed=1000, transcendentals=0)
MEDIUM = pl.CostEstimate(flops=1 << 32, bytes_accessed=1000, transcendentals=0)
LONG = pl.CostEstimate(flops=1 << 34, bytes_accessed=MIB, transcendentals=0)


def positions(lengths, token_index):
    doc_ends = jnp.cumsum(lengths, axis=1)
    doc_start = jnp.max(jnp.where(doc_ends <= token_index[:, None], doc_ends, 0), axis=1)
    return token_index - doc_start


def kva_rows_grad(stacked, latent, norm_gain, position):
    width = latent.shape[1]
    latent_part = stacked[:, :width]
    rotary_part = stacked[:, width:]
    values = latent.astype(F32)
    inverse_rms = lax.rsqrt(jnp.mean(values * values, axis=1, keepdims=True) + 1e-06)
    scaled_grad = latent_part * norm_gain[None, :]
    norm_grad = inverse_rms * (
        scaled_grad
        - values * inverse_rms * inverse_rms * jnp.mean(scaled_grad * values, axis=1, keepdims=True)
    )
    half_width = rotary_part.shape[1] // 2
    inv_freq = 10000.0 ** (-(2.0 * jnp.arange(half_width, dtype=F32)) / (2.0 * half_width))
    angles = position.astype(F32)[:, None] * inv_freq[None, :]
    cosine = jnp.cos(angles)
    sine = jnp.sin(angles)
    first_half = rotary_part[:, :half_width]
    second_half = rotary_part[:, half_width:]
    rot_first = first_half * cosine + second_half * sine
    rot_second = second_half * cosine - first_half * sine
    return jnp.concatenate([norm_grad, rot_first, rot_second], axis=1).astype(BF16)


def on_device_any(
    key_grad, value_grad, rope_grad, key_lift, value_lift, latent, norm_gain, doc_lengths, hidden, down_proj
):
    seq_len = key_grad.shape[0]
    rope = down_proj.shape[1] - latent.shape[1]
    head_terms = lax.dot_general(key_grad, key_lift, LAST, preferred_element_type=F32)
    head_terms = head_terms + lax.dot_general(value_grad, value_lift, LAST, preferred_element_type=F32)
    heads_here = rope_grad.shape[1] // rope
    rope_terms = jnp.sum(rope_grad.reshape(seq_len, heads_here, rope), axis=1, dtype=F32)
    stacked = jnp.concatenate([head_terms, rope_terms], axis=1)
    shared = lax.psum_scatter(stacked, "head", scatter_dimension=0, tiled=True)
    share_rows = shared.shape[0]
    first_row = lax.axis_index("head") * share_rows
    own_latent = lax.dynamic_slice_in_dim(latent, first_row, share_rows, 0)
    token_index = first_row + jnp.arange(share_rows, dtype=jnp.int32)
    row_lengths = jnp.broadcast_to(doc_lengths, (share_rows, doc_lengths.shape[1]))
    own_grad = kva_rows_grad(shared, own_latent, norm_gain, positions(row_lengths, token_index))
    kva_grad = lax.all_gather(own_grad, "head", axis=0, tiled=True)
    hidden_grad = lax.dot_general(kva_grad, down_proj, LAST, preferred_element_type=F32).astype(BF16)
    weight_grad = lax.psum_scatter(
        lax.dot_general(kva_grad, hidden, FIRST, preferred_element_type=F32),
        "group",
        scatter_dimension=0,
        tiled=True,
    )
    return (hidden_grad, weight_grad)


def axis_bits():
    return 1, 2, 4


def after(array, other):
    return lax.optimization_barrier((array, other))


def row_order(blocks):
    core, x, y = axis_bits()
    mine = lax.axis_index("group")
    first = jnp.where(mine & core == 0, x, y)
    other, second, both = mine ^ core, first ^ (x | y), x | y
    order = [mine ^ both, other ^ both]
    order += [mine ^ first, mine ^ second, mine, other ^ second, other ^ first, other]
    assert len(order) == blocks
    return order


def partial_kernel(*refs, which, dtypes, rope, block, chunks, lifts_here):
    count = len(which)
    lengths, kg, vg, rg, kl, vl, lat, gain = refs[:8]
    outs, refs = refs[8 : 8 + count], refs[8 + count :]
    if lifts_here:
        kl_v, vl_v = kl, vl
    else:
        (kl_v, vl_v), refs = refs[:2], refs[2:]
    kg_v, vg_v, rg_v, lat_v, gain_v, lengths_s, sems, acc, rope_acc, values, turns, rows = refs
    share = outs[0].shape[1]
    latent = lat.shape[1]
    half = rope // 2
    shares = [lax.axis_index("head") ^ r for r in which]
    places = [pl.ds(pl.multiple_of(r * share, share), share) for r in shares]
    sides = [slice(side * share, (side + 1) * share) for side in range(count)]

    def columns(ref, chunk):
        width = ref.shape[1] // chunks
        return slice(chunk * width, (chunk + 1) * width)

    def copies_of(chunk):
        pairs = []
        if not lifts_here:
            for src, dst in ((kl, kl_v), (vl, vl_v)):
                pairs.append((src.at[:, columns(src, chunk)], dst.at[:, columns(src, chunk)]))
        for src, dst in ((kg, kg_v), (vg, vg_v), (rg, rg_v)):
            for place, side in zip(places, sides):
                pairs.append((src.at[place, columns(src, chunk)], dst.at[side, columns(src, chunk)]))
        return [pltpu.make_async_copy(src, dst, sems.at[chunk, i]) for i, (src, dst) in enumerate(pairs)]

    small = [(lat.at[place, :], lat_v.at[side, :]) for place, side in zip(places, sides)]
    small += [(gain, gain_v), (lengths, lengths_s)]
    small_copies = [pltpu.make_async_copy(src, dst, sems.at[chunks, i]) for i, (src, dst) in enumerate(small)]
    all_copies = [copies_of(chunk) for chunk in range(chunks)]
    for copy in all_copies[0] + small_copies + [copy for copies in all_copies[1:] for copy in copies]:
        copy.start()

    fold_shape = (rope, rg.shape[1] // chunks)
    fold = lax.rem(lax.broadcasted_iota(jnp.int32, fold_shape, 1), rope) == lax.broadcasted_iota(
        jnp.int32, fold_shape, 0
    )
    fold = fold.astype(BF16)

    for chunk in range(chunks):
        for copy in all_copies[chunk]:
            copy.wait()
        here = columns(kg, chunk)
        term = lax.dot_general(kg_v[:, here], kl_v[:, here], LAST, preferred_element_type=F32)
        term += lax.dot_general(vg_v[:, here], vl_v[:, here], LAST, preferred_element_type=F32)
        rope_term = lax.dot_general(fold, rg_v[:, columns(rg, chunk)], LAST, preferred_element_type=F32)
        acc[...] = term if chunk == 0 else acc[...] + term
        rope_acc[...] = rope_term if chunk == 0 else rope_acc[...] + rope_term
        if chunk == 0:
            for copy in small_copies:
                copy.wait()
            values[...] = lat_v[...].astype(F32).T
            lane = lax.broadcasted_iota(jnp.int32, (1, share), 1)
            pair = lax.broadcasted_iota(jnp.int32, (half, share), 0).astype(F32)
            freq = jnp.exp(pair * (-math.log(10000.0) / half))
            for r, side in zip(shares, sides):
                token = r * share + lane
                start = jnp.zeros_like(token)
                end = jnp.int32(0)
                for doc in range(lengths.shape[1]):
                    end = end + lengths_s[0, doc]
                    start = jnp.maximum(start, jnp.where(end <= token, end, 0))
                angle = (token - start).astype(F32) * freq
                turns[:half, side] = jnp.cos(angle)
                turns[half:, side] = jnp.sin(angle)

    gains = jnp.broadcast_to(gain_v[...], (share, latent)).T
    gains = jnp.concatenate([gains] * count, axis=1)
    c = values[...]
    inv = lax.rsqrt(jnp.mean(c * c, axis=0, keepdims=True) + 1e-06)
    g = acc[...].T * gains
    mean = jnp.mean(g * c, axis=0, keepdims=True)
    rows[:latent, :] = inv * (g - c * (inv * inv * mean))
    first, second = rope_acc[:half, :], rope_acc[half:, :]
    rows[latent : latent + half, :] = first * turns[:half, :] + second * turns[half:, :]
    rows[latent + half :, :] = second * turns[:half, :] - first * turns[half:, :]
    ordered = jnp.concatenate(
        [rows[pl.ds(pl.multiple_of(r * block, 8), block), :] for r in row_order(rows.shape[0] // block)], axis=0
    )
    for out, dtype, side in zip(outs, dtypes, sides):
        out[...] = ordered[:, side].astype(dtype)


def partial_terms(which, dtypes, doc_lengths, kg, vg, rg, kl, vl, latent, gain, share, rope, block, lifts_here):
    key_cols = kg.shape[1]
    width = latent.shape[1]
    kva = width + rope
    tokens = len(which) * share
    chunks = 4 if lifts_here else 8
    if key_cols % (chunks * 128) or rg.shape[1] % (chunks * 128):
        chunks = 1
    operands = (doc_lengths, kg, vg, rg, kl, vl, latent, gain)
    spaces = [pltpu.VMEM if lifts_here and i in (4, 5) else pltpu.HBM for i in range(len(operands))]
    out_shape = [pltpu.VMEM((kva, share), dtype) for dtype in dtypes]
    if not lifts_here:
        out_shape += [pltpu.VMEM(kl.shape, BF16), pltpu.VMEM(vl.shape, BF16)]
    return pl.pallas_call(
        functools.partial(
            partial_kernel, which=which, dtypes=dtypes, rope=rope, block=block, chunks=chunks, lifts_here=lifts_here
        ),
        in_specs=[pl.BlockSpec(memory_space=space) for space in spaces],
        out_specs=[pl.BlockSpec(memory_space=pltpu.VMEM)] * len(out_shape),
        scratch_shapes=[
            pltpu.VMEM((tokens, key_cols), BF16),
            pltpu.VMEM((tokens, key_cols), BF16),
            pltpu.VMEM((tokens, rg.shape[1]), BF16),
            pltpu.VMEM((tokens, width), BF16),
            pltpu.VMEM(gain.shape, F32),
            pltpu.SMEM(doc_lengths.shape, jnp.int32),
            pltpu.SemaphoreType.DMA((chunks + 1, 2 + 3 * len(which))),
            pltpu.VMEM((tokens, width), F32),
            pltpu.VMEM((rope, tokens), F32),
            pltpu.VMEM((width, tokens), F32),
            pltpu.VMEM((rope, tokens), F32),
            pltpu.VMEM((kva, tokens), F32),
        ],
        out_shape=out_shape,
        compiler_params=pltpu.CompilerParams(vmem_limit_bytes=28 * MIB),
        cost_estimate=LONG,
        name="partial_terms",
    )(*[pltpu.with_memory_space_constraint(x, space) for x, space in zip(operands, spaces)])


def weight_kernel(*refs, skips):
    shares, hidden, sibling_hidden, outs = refs[:8], refs[8], refs[9], refs[10:]
    share = shares[0].shape[1]
    block = outs[0].shape[0]
    count = len(outs) * block

    def rows_of(ref, skip, side):
        return ref[skip : skip + 2 * count].astype(F32)[side * count : (side + 1) * count]

    left = [rows_of(ref, skip, i // 4) for i, (ref, skip) in enumerate(zip(shares, skips))]
    left = jnp.concatenate(left, axis=1).astype(BF16)
    columns = hidden.shape[1]
    width = 256 if columns % 256 == 0 else columns
    me = lax.axis_index("head")
    places = [pl.ds(pl.multiple_of((me ^ r) * share, share), share) for r in range(4)]
    for n in range(columns // width):
        cols = slice(n * width, (n + 1) * width)
        right = [ref[place, cols] for ref in (hidden, sibling_hidden) for place in places]
        result = jnp.dot(left, jnp.concatenate(right, axis=0), preferred_element_type=F32)
        for i, out in enumerate(outs):
            out[:, cols] = result[i * block : (i + 1) * block].astype(out.dtype)


def weight_terms(shares, skips, hidden, sibling_hidden, block, dtypes):
    columns = hidden.shape[1]
    vmem = pl.BlockSpec(memory_space=pltpu.VMEM)
    operands = (*shares, hidden, sibling_hidden)
    return pl.pallas_call(
        functools.partial(weight_kernel, skips=skips),
        in_specs=[vmem] * len(operands),
        out_specs=[vmem] * len(dtypes),
        out_shape=[pltpu.VMEM((block, columns), dtype) for dtype in dtypes],
        compiler_params=pltpu.CompilerParams(vmem_limit_bytes=24 * MIB),
        cost_estimate=SHORT,
        name="weight_terms",
    )(*[pltpu.with_memory_space_constraint(x, pltpu.VMEM) for x in operands])


def natural_kernel(*refs, block):
    even_a, odd_a, even_b, odd_b, out, natural = refs
    head, rest = even_a.shape[0] // 2, even_b.shape[0] // 2
    parts = [(ahead[:head], then[:rest]) for ahead, then in ((even_a, even_b), (odd_a, odd_b))]
    parts += [(ahead[head:], then[rest:]) for ahead, then in ((even_a, even_b), (odd_a, odd_b))]
    me = lax.axis_index("head")
    order = row_order(natural.shape[0] // block)
    share = natural.shape[1]
    for r, pieces in enumerate(parts):
        ordered = jnp.concatenate([piece.astype(F32) for piece in pieces], axis=0)
        for i, place in enumerate(order):
            natural[pl.ds(pl.multiple_of(place * block, 8), block), :] = ordered[i * block : (i + 1) * block]
        out[pl.ds(pl.multiple_of((me ^ r) * share, share), share), :] = natural[...].T.astype(BF16)


def natural_rows(parts, block):
    kva, share = sum(part.shape[0] for part in parts) // 4, parts[0].shape[1]
    return pl.pallas_call(
        functools.partial(natural_kernel, block=block),
        in_specs=[pl.BlockSpec(memory_space=pltpu.VMEM)] * len(parts),
        out_specs=pl.BlockSpec(memory_space=pltpu.VMEM),
        scratch_shapes=[pltpu.VMEM((kva, share), F32)],
        out_shape=pltpu.VMEM((4 * share, kva), BF16),
        compiler_params=pltpu.CompilerParams(vmem_limit_bytes=24 * MIB),
        cost_estimate=SHORT,
        name="natural_rows",
    )(*[pltpu.with_memory_space_constraint(x, pltpu.VMEM) for x in parts])


def add_kernel(*refs, starts, waits):
    outs = refs[len(starts) + waits :]
    at = 0
    for out in outs:
        rows = out.shape[0]
        total = sum(ref[start + at : start + at + rows].astype(F32) for ref, start in zip(refs, starts))
        out[...] = total.astype(out.dtype)
        at += rows


def add_rows(terms, starts, outs, waits=()):
    columns = terms[0].shape[1]
    vmem = pl.BlockSpec(memory_space=pltpu.VMEM)
    return pl.pallas_call(
        functools.partial(add_kernel, starts=starts, waits=len(waits)),
        in_specs=[vmem] * len(terms) + [pl.BlockSpec(memory_space=pl.ANY)] * len(waits),
        out_specs=[vmem] * len(outs),
        out_shape=[pltpu.VMEM((rows, columns), dtype) for rows, dtype in outs],
        compiler_params=pltpu.CompilerParams(vmem_limit_bytes=24 * MIB),
        cost_estimate=LONG,
        name="add_rows",
    )(*[pltpu.with_memory_space_constraint(x, pltpu.VMEM) for x in terms], *waits)


def stack_kernel(*refs, count):
    out, at = refs[-1], 0
    for ref in refs[:count]:
        out[at : at + ref.shape[0]] = ref[...]
        at += ref.shape[0]


def stack(arrays, *waits, cost=None):
    rows = sum(array.shape[0] for array in arrays)
    vmem = pl.BlockSpec(memory_space=pltpu.VMEM)
    return pl.pallas_call(
        functools.partial(stack_kernel, count=len(arrays)),
        in_specs=[vmem] * len(arrays) + [pl.BlockSpec(memory_space=pl.ANY)] * len(waits),
        out_specs=vmem,
        out_shape=pltpu.VMEM((rows, arrays[0].shape[1]), arrays[0].dtype),
        compiler_params=pltpu.CompilerParams(vmem_limit_bytes=24 * MIB),
        cost_estimate=cost or LONG,
        name="stack",
    )(*[pltpu.with_memory_space_constraint(x, pltpu.VMEM) for x in arrays], *waits)


def hidden_kernel(rows, down_t, out):
    out[...] = jnp.dot(rows[...], down_t[...], preferred_element_type=F32).astype(out.dtype)


def hidden_terms(rows, down_t):
    tokens = rows.shape[0]
    kva, columns = down_t.shape
    col_block = columns // 2 if columns % 256 == 0 else columns
    return pl.pallas_call(
        hidden_kernel,
        grid=(columns // col_block,),
        in_specs=[pl.BlockSpec((tokens, kva), lambda n: (0, 0)), pl.BlockSpec((kva, col_block), lambda n: (0, n))],
        out_specs=pl.BlockSpec((tokens, col_block), lambda n: (0, n)),
        out_shape=jax.ShapeDtypeStruct((tokens, columns), BF16),
        compiler_params=pltpu.CompilerParams(vmem_limit_bytes=24 * MIB),
        cost_estimate=LONG,
        name="hidden_terms",
    )(rows, down_t)


def on_device(
    key_grad, value_grad, rope_grad, key_lift, value_lift, latent, norm_gain, doc_lengths, hidden, down_proj
):
    heads, groups = 4, 8
    core_bit, x_bit, y_bit = axis_bits()
    share = key_grad.shape[0] // heads
    kva = down_proj.shape[1]
    block = kva // groups

    def swap_head(array, bits):
        return lax.ppermute(array, "head", [(i, i ^ bits) for i in range(heads)])

    def swap_group(array, bits_of):
        return lax.ppermute(array, "group", [(i, i ^ bits_of(i)) for i in range(groups)])

    def swap_core(array):
        return swap_group(array, lambda i: core_bit)

    def first_bit(i):
        return y_bit if i & core_bit else x_bit

    def second_bit(i):
        return x_bit if i & core_bit else y_bit

    gain = norm_gain.reshape(1, -1)
    def terms(which, dtypes, lifts, lifts_here):
        return partial_terms(
            which, dtypes, doc_lengths, key_grad, value_grad, rope_grad, *lifts,
            latent, gain, share, kva - latent.shape[1], block, lifts_here,
        )

    p3, *lifts = terms((3,), (BF16,), (key_lift, value_lift), False)
    got3 = swap_head(p3, 1)
    p2, p1 = terms((2, 1), (F32, BF16), lifts, True)
    (pair2,) = add_rows((p2, got3), (0, 0), [(kva, BF16)])
    pair2, p1, hidden, *lifts = lax.optimization_barrier((pair2, p1, hidden, *lifts))
    got2 = swap_head(pair2, 2)
    got1 = swap_head(p1, 1)
    sibling_hidden = swap_core(hidden)
    (p0,) = terms((0,), (F32,), lifts, True)
    ahead, rest = 2 * block, kva - 2 * block
    (q0_a,) = add_rows((p0, got1, got2), (0, 0, 0), [(ahead, BF16)])
    (q0_b,) = add_rows((p0, got1, got2), (ahead,) * 3, [(rest, BF16)], (q0_a,))
    q2_a, q2_b = swap_head(q0_a, 2), swap_head(q0_b, 2)
    even_a = stack((q0_a, q2_a))
    odd_a = swap_head(even_a, 1)
    q1_b = swap_head(stack((q0_b,), even_a, cost=SHORT), 1)
    q2_b = stack((q2_b,), even_a)
    q3_b = swap_head(q2_b, 1)
    odd_a = stack((odd_a,), q2_b, cost=MEDIUM)
    even_b = stack((q0_b, q2_b), cost=SHORT)

    def weights(even, odd, dtypes):
        shares = (even, odd) * 2 + (swap_core(even), swap_core(odd)) * 2
        half = even.shape[0] // 2
        return weight_terms(shares, (0, 0, half, half) * 2, hidden, sibling_hidden, block, dtypes)

    (for_both,) = weights(even_a, odd_a, (BF16,))
    got_both = swap_group(for_both, first_bit)
    odd_b = stack((q1_b, q3_b), for_both)
    for_first, for_second, mine = weights(even_b, odd_b, (BF16, F32, F32))
    got_first = swap_group(for_first, first_bit)
    kva_rows = natural_rows((even_a, odd_a, even_b, odd_b), block)
    (to_second,) = add_rows((for_second, got_both), (0, 0), [(block, BF16)], (kva_rows,))
    got_second = swap_group(to_second, second_bit)
    kva_rows, to_second = after(kva_rows, to_second)
    hidden_grad = hidden_terms(kva_rows, down_proj.T)
    weight_grad = mine + got_first.astype(F32) + got_second.astype(F32)
    return (hidden_grad, weight_grad)


def solution(mesh):
    shape = dict(mesh.shape)
    paired = shape["head"] == 4 and shape["group"] == 8
    return jax.shard_map(
        on_device if paired else on_device_any,
        mesh=mesh,
        in_specs=(
            P("group", "head"),
            P("group", "head"),
            P("group", "head"),
            P(None, "head"),
            P(None, "head"),
            P("group", None),
            P(),
            P("group", None),
            P("group", "head"),
            P("head", None),
        ),
        out_specs=(P("group", "head"), P("group", "head")),
        check_vma=False,
    )
```

```python
import functools
import math

import jax
import jax.numpy as jnp
from jax import lax
from jax.experimental import pallas as pl
from jax.experimental.pallas import tpu as pltpu
from jax.sharding import PartitionSpec as P

F32 = jnp.float32
BF16 = jnp.bfloat16
LAST = (((1,), (1,)), ((), ()))
FIRST = (((0,), (0,)), ((), ()))
MIB = 1 << 20
SHORT = pl.CostEstimate(flops=1000, bytes_accessed=1000, transcendentals=0)
MEDIUM = pl.CostEstimate(flops=1 << 32, bytes_accessed=1000, transcendentals=0)
LONG = pl.CostEstimate(flops=1 << 34, bytes_accessed=MIB, transcendentals=0)


def positions(lengths, token_index):
    doc_ends = jnp.cumsum(lengths, axis=1)
    doc_start = jnp.max(jnp.where(doc_ends <= token_index[:, None], doc_ends, 0), axis=1)
    return token_index - doc_start


def kva_rows_grad(stacked, latent, norm_gain, position):
    width = latent.shape[1]
    latent_part = stacked[:, :width]
    rotary_part = stacked[:, width:]
    values = latent.astype(F32)
    inverse_rms = lax.rsqrt(jnp.mean(values * values, axis=1, keepdims=True) + 1e-06)
    scaled_grad = latent_part * norm_gain[None, :]
    norm_grad = inverse_rms * (
        scaled_grad
        - values * inverse_rms * inverse_rms * jnp.mean(scaled_grad * values, axis=1, keepdims=True)
    )
    half_width = rotary_part.shape[1] // 2
    inv_freq = 10000.0 ** (-(2.0 * jnp.arange(half_width, dtype=F32)) / (2.0 * half_width))
    angles = position.astype(F32)[:, None] * inv_freq[None, :]
    cosine = jnp.cos(angles)
    sine = jnp.sin(angles)
    first_half = rotary_part[:, :half_width]
    second_half = rotary_part[:, half_width:]
    rot_first = first_half * cosine + second_half * sine
    rot_second = second_half * cosine - first_half * sine
    return jnp.concatenate([norm_grad, rot_first, rot_second], axis=1).astype(BF16)


def on_device_any(
    key_grad, value_grad, rope_grad, key_lift, value_lift, latent, norm_gain, doc_lengths, hidden, down_proj
):
    seq_len = key_grad.shape[0]
    rope = down_proj.shape[1] - latent.shape[1]
    head_terms = lax.dot_general(key_grad, key_lift, LAST, preferred_element_type=F32)
    head_terms = head_terms + lax.dot_general(value_grad, value_lift, LAST, preferred_element_type=F32)
    heads_here = rope_grad.shape[1] // rope
    rope_terms = jnp.sum(rope_grad.reshape(seq_len, heads_here, rope), axis=1, dtype=F32)
    stacked = jnp.concatenate([head_terms, rope_terms], axis=1)
    shared = lax.psum_scatter(stacked, "head", scatter_dimension=0, tiled=True)
    share_rows = shared.shape[0]
    first_row = lax.axis_index("head") * share_rows
    own_latent = lax.dynamic_slice_in_dim(latent, first_row, share_rows, 0)
    token_index = first_row + jnp.arange(share_rows, dtype=jnp.int32)
    row_lengths = jnp.broadcast_to(doc_lengths, (share_rows, doc_lengths.shape[1]))
    own_grad = kva_rows_grad(shared, own_latent, norm_gain, positions(row_lengths, token_index))
    kva_grad = lax.all_gather(own_grad, "head", axis=0, tiled=True)
    hidden_grad = lax.dot_general(kva_grad, down_proj, LAST, preferred_element_type=F32).astype(BF16)
    weight_grad = lax.psum_scatter(
        lax.dot_general(kva_grad, hidden, FIRST, preferred_element_type=F32),
        "group",
        scatter_dimension=0,
        tiled=True,
    )
    return (hidden_grad, weight_grad)


def axis_bits():
    return 1, 2, 4


def after(array, other):
    return lax.optimization_barrier((array, other))


def row_order(blocks):
    core, x, y = axis_bits()
    mine = lax.axis_index("group")
    first = jnp.where(mine & core == 0, x, y)
    other, second, both = mine ^ core, first ^ (x | y), x | y
    order = [mine ^ both, other ^ both]
    order += [mine ^ first, mine ^ second, mine, other ^ second, other ^ first, other]
    assert len(order) == blocks
    return order


def partial_kernel(*refs, which, dtypes, rope, block, chunks, lifts_here):
    count = len(which)
    lengths, kg, vg, rg, kl, vl, lat, gain = refs[:8]
    outs, refs = refs[8 : 8 + count], refs[8 + count :]
    if lifts_here:
        kl_v, vl_v = kl, vl
    else:
        (kl_v, vl_v), refs = refs[:2], refs[2:]
    kg_v, vg_v, rg_v, lat_v, gain_v, lengths_s, sems, acc, rope_acc, values, turns, rows = refs
    share = outs[0].shape[1]
    latent = lat.shape[1]
    half = rope // 2
    shares = [lax.axis_index("head") ^ r for r in which]
    places = [pl.ds(pl.multiple_of(r * share, share), share) for r in shares]
    sides = [slice(side * share, (side + 1) * share) for side in range(count)]

    def columns(ref, chunk):
        width = ref.shape[1] // chunks
        return slice(chunk * width, (chunk + 1) * width)

    def copies_of(chunk):
        pairs = []
        if not lifts_here:
            for src, dst in ((kl, kl_v), (vl, vl_v)):
                pairs.append((src.at[:, columns(src, chunk)], dst.at[:, columns(src, chunk)]))
        for src, dst in ((kg, kg_v), (vg, vg_v), (rg, rg_v)):
            for place, side in zip(places, sides):
                pairs.append((src.at[place, columns(src, chunk)], dst.at[side, columns(src, chunk)]))
        return [pltpu.make_async_copy(src, dst, sems.at[chunk, i]) for i, (src, dst) in enumerate(pairs)]

    small = [(lat.at[place, :], lat_v.at[side, :]) for place, side in zip(places, sides)]
    small += [(gain, gain_v), (lengths, lengths_s)]
    small_copies = [pltpu.make_async_copy(src, dst, sems.at[chunks, i]) for i, (src, dst) in enumerate(small)]
    all_copies = [copies_of(chunk) for chunk in range(chunks)]
    for copy in all_copies[0] + small_copies + [copy for copies in all_copies[1:] for copy in copies]:
        copy.start()

    fold_shape = (rope, rg.shape[1] // chunks)
    fold = lax.rem(lax.broadcasted_iota(jnp.int32, fold_shape, 1), rope) == lax.broadcasted_iota(
        jnp.int32, fold_shape, 0
    )
    fold = fold.astype(BF16)

    for chunk in range(chunks):
        for copy in all_copies[chunk]:
            copy.wait()
        here = columns(kg, chunk)
        term = lax.dot_general(kg_v[:, here], kl_v[:, here], LAST, preferred_element_type=F32)
        term += lax.dot_general(vg_v[:, here], vl_v[:, here], LAST, preferred_element_type=F32)
        rope_term = lax.dot_general(fold, rg_v[:, columns(rg, chunk)], LAST, preferred_element_type=F32)
        acc[...] = term if chunk == 0 else acc[...] + term
        rope_acc[...] = rope_term if chunk == 0 else rope_acc[...] + rope_term
        if chunk == 0:
            for copy in small_copies:
                copy.wait()
            values[...] = lat_v[...].astype(F32).T
            lane = lax.broadcasted_iota(jnp.int32, (1, share), 1)
            pair = lax.broadcasted_iota(jnp.int32, (half, share), 0).astype(F32)
            freq = jnp.exp(pair * (-math.log(10000.0) / half))
            for r, side in zip(shares, sides):
                token = r * share + lane
                start = jnp.zeros_like(token)
                end = jnp.int32(0)
                for doc in range(lengths.shape[1]):
                    end = end + lengths_s[0, doc]
                    start = jnp.maximum(start, jnp.where(end <= token, end, 0))
                angle = (token - start).astype(F32) * freq
                turns[:half, side] = jnp.cos(angle)
                turns[half:, side] = jnp.sin(angle)

    gains = jnp.broadcast_to(gain_v[...], (share, latent)).T
    gains = jnp.concatenate([gains] * count, axis=1)
    c = values[...]
    inv = lax.rsqrt(jnp.mean(c * c, axis=0, keepdims=True) + 1e-06)
    g = acc[...].T * gains
    mean = jnp.mean(g * c, axis=0, keepdims=True)
    rows[:latent, :] = inv * (g - c * (inv * inv * mean))
    first, second = rope_acc[:half, :], rope_acc[half:, :]
    rows[latent : latent + half, :] = first * turns[:half, :] + second * turns[half:, :]
    rows[latent + half :, :] = second * turns[:half, :] - first * turns[half:, :]
    ordered = jnp.concatenate(
        [rows[pl.ds(pl.multiple_of(r * block, 8), block), :] for r in row_order(rows.shape[0] // block)], axis=0
    )
    for out, dtype, side in zip(outs, dtypes, sides):
        out[...] = ordered[:, side].astype(dtype)


def partial_terms(which, dtypes, doc_lengths, kg, vg, rg, kl, vl, latent, gain, share, rope, block, lifts_here):
    key_cols = kg.shape[1]
    width = latent.shape[1]
    kva = width + rope
    tokens = len(which) * share
    chunks = 2 if lifts_here else 8
    if key_cols % (chunks * 128) or rg.shape[1] % (chunks * 128):
        chunks = 1
    operands = (doc_lengths, kg, vg, rg, kl, vl, latent, gain)
    spaces = [pltpu.VMEM if lifts_here and i in (4, 5) else pltpu.HBM for i in range(len(operands))]
    out_shape = [pltpu.VMEM((kva, share), dtype) for dtype in dtypes]
    if not lifts_here:
        out_shape += [pltpu.VMEM(kl.shape, BF16), pltpu.VMEM(vl.shape, BF16)]
    return pl.pallas_call(
        functools.partial(
            partial_kernel, which=which, dtypes=dtypes, rope=rope, block=block, chunks=chunks, lifts_here=lifts_here
        ),
        in_specs=[pl.BlockSpec(memory_space=space) for space in spaces],
        out_specs=[pl.BlockSpec(memory_space=pltpu.VMEM)] * len(out_shape),
        scratch_shapes=[
            pltpu.VMEM((tokens, key_cols), BF16),
            pltpu.VMEM((tokens, key_cols), BF16),
            pltpu.VMEM((tokens, rg.shape[1]), BF16),
            pltpu.VMEM((tokens, width), BF16),
            pltpu.VMEM(gain.shape, F32),
            pltpu.SMEM(doc_lengths.shape, jnp.int32),
            pltpu.SemaphoreType.DMA((chunks + 1, 2 + 3 * len(which))),
            pltpu.VMEM((tokens, width), F32),
            pltpu.VMEM((rope, tokens), F32),
            pltpu.VMEM((width, tokens), F32),
            pltpu.VMEM((rope, tokens), F32),
            pltpu.VMEM((kva, tokens), F32),
        ],
        out_shape=out_shape,
        compiler_params=pltpu.CompilerParams(vmem_limit_bytes=28 * MIB),
        cost_estimate=LONG,
        name="partial_terms",
    )(*[pltpu.with_memory_space_constraint(x, space) for x, space in zip(operands, spaces)])


def weight_kernel(*refs, skips):
    shares, hidden, sibling_hidden, outs = refs[:8], refs[8], refs[9], refs[10:]
    share = shares[0].shape[1]
    block = outs[0].shape[0]
    count = len(outs) * block

    def rows_of(ref, skip, side):
        return ref[skip : skip + 2 * count].astype(F32)[side * count : (side + 1) * count]

    left = [rows_of(ref, skip, i // 4) for i, (ref, skip) in enumerate(zip(shares, skips))]
    left = jnp.concatenate(left, axis=1).astype(BF16)
    columns = hidden.shape[1]
    width = 256 if columns % 256 == 0 else columns
    me = lax.axis_index("head")
    places = [pl.ds(pl.multiple_of((me ^ r) * share, share), share) for r in range(4)]
    for n in range(columns // width):
        cols = slice(n * width, (n + 1) * width)
        right = [ref[place, cols] for ref in (hidden, sibling_hidden) for place in places]
        result = jnp.dot(left, jnp.concatenate(right, axis=0), preferred_element_type=F32)
        for i, out in enumerate(outs):
            out[:, cols] = result[i * block : (i + 1) * block].astype(out.dtype)


def weight_terms(shares, skips, hidden, sibling_hidden, block, dtypes):
    columns = hidden.shape[1]
    vmem = pl.BlockSpec(memory_space=pltpu.VMEM)
    operands = (*shares, hidden, sibling_hidden)
    return pl.pallas_call(
        functools.partial(weight_kernel, skips=skips),
        in_specs=[vmem] * len(operands),
        out_specs=[vmem] * len(dtypes),
        out_shape=[pltpu.VMEM((block, columns), dtype) for dtype in dtypes],
        compiler_params=pltpu.CompilerParams(vmem_limit_bytes=24 * MIB),
        cost_estimate=SHORT,
        name="weight_terms",
    )(*[pltpu.with_memory_space_constraint(x, pltpu.VMEM) for x in operands])


def natural_kernel(*refs, block):
    even_a, odd_a, even_b, odd_b, out, natural = refs
    head, rest = even_a.shape[0] // 2, even_b.shape[0] // 2
    parts = [(ahead[:head], then[:rest]) for ahead, then in ((even_a, even_b), (odd_a, odd_b))]
    parts += [(ahead[head:], then[rest:]) for ahead, then in ((even_a, even_b), (odd_a, odd_b))]
    me = lax.axis_index("head")
    order = row_order(natural.shape[0] // block)
    share = natural.shape[1]
    for r, pieces in enumerate(parts):
        ordered = jnp.concatenate([piece.astype(F32) for piece in pieces], axis=0)
        for i, place in enumerate(order):
            natural[pl.ds(pl.multiple_of(place * block, 8), block), :] = ordered[i * block : (i + 1) * block]
        out[pl.ds(pl.multiple_of((me ^ r) * share, share), share), :] = natural[...].T.astype(BF16)


def natural_rows(parts, block):
    kva, share = sum(part.shape[0] for part in parts) // 4, parts[0].shape[1]
    return pl.pallas_call(
        functools.partial(natural_kernel, block=block),
        in_specs=[pl.BlockSpec(memory_space=pltpu.VMEM)] * len(parts),
        out_specs=pl.BlockSpec(memory_space=pltpu.VMEM),
        scratch_shapes=[pltpu.VMEM((kva, share), F32)],
        out_shape=pltpu.VMEM((4 * share, kva), BF16),
        compiler_params=pltpu.CompilerParams(vmem_limit_bytes=24 * MIB),
        cost_estimate=SHORT,
        name="natural_rows",
    )(*[pltpu.with_memory_space_constraint(x, pltpu.VMEM) for x in parts])


def add_kernel(*refs, starts, waits):
    outs = refs[len(starts) + waits :]
    at = 0
    for out in outs:
        rows = out.shape[0]
        total = sum(ref[start + at : start + at + rows].astype(F32) for ref, start in zip(refs, starts))
        out[...] = total.astype(out.dtype)
        at += rows


def add_rows(terms, starts, outs, waits=()):
    columns = terms[0].shape[1]
    vmem = pl.BlockSpec(memory_space=pltpu.VMEM)
    return pl.pallas_call(
        functools.partial(add_kernel, starts=starts, waits=len(waits)),
        in_specs=[vmem] * len(terms) + [pl.BlockSpec(memory_space=pl.ANY)] * len(waits),
        out_specs=[vmem] * len(outs),
        out_shape=[pltpu.VMEM((rows, columns), dtype) for rows, dtype in outs],
        compiler_params=pltpu.CompilerParams(vmem_limit_bytes=24 * MIB),
        cost_estimate=LONG,
        name="add_rows",
    )(*[pltpu.with_memory_space_constraint(x, pltpu.VMEM) for x in terms], *waits)


def stack_kernel(*refs, count):
    out, at = refs[-1], 0
    for ref in refs[:count]:
        out[at : at + ref.shape[0]] = ref[...]
        at += ref.shape[0]


def stack(arrays, *waits, cost=None):
    rows = sum(array.shape[0] for array in arrays)
    vmem = pl.BlockSpec(memory_space=pltpu.VMEM)
    return pl.pallas_call(
        functools.partial(stack_kernel, count=len(arrays)),
        in_specs=[vmem] * len(arrays) + [pl.BlockSpec(memory_space=pl.ANY)] * len(waits),
        out_specs=vmem,
        out_shape=pltpu.VMEM((rows, arrays[0].shape[1]), arrays[0].dtype),
        compiler_params=pltpu.CompilerParams(vmem_limit_bytes=24 * MIB),
        cost_estimate=cost or LONG,
        name="stack",
    )(*[pltpu.with_memory_space_constraint(x, pltpu.VMEM) for x in arrays], *waits)


def hidden_kernel(rows, down_t, out):
    out[...] = jnp.dot(rows[...], down_t[...], preferred_element_type=F32).astype(out.dtype)


def hidden_terms(rows, down_t):
    tokens = rows.shape[0]
    kva, columns = down_t.shape
    col_block = columns // 2 if columns % 256 == 0 else columns
    return pl.pallas_call(
        hidden_kernel,
        grid=(columns // col_block,),
        in_specs=[pl.BlockSpec((tokens, kva), lambda n: (0, 0)), pl.BlockSpec((kva, col_block), lambda n: (0, n))],
        out_specs=pl.BlockSpec((tokens, col_block), lambda n: (0, n)),
        out_shape=jax.ShapeDtypeStruct((tokens, columns), BF16),
        compiler_params=pltpu.CompilerParams(vmem_limit_bytes=24 * MIB),
        cost_estimate=LONG,
        name="hidden_terms",
    )(rows, down_t)


def on_device(
    key_grad, value_grad, rope_grad, key_lift, value_lift, latent, norm_gain, doc_lengths, hidden, down_proj
):
    heads, groups = 4, 8
    core_bit, x_bit, y_bit = axis_bits()
    share = key_grad.shape[0] // heads
    kva = down_proj.shape[1]
    block = kva // groups

    def swap_head(array, bits):
        return lax.ppermute(array, "head", [(i, i ^ bits) for i in range(heads)])

    def swap_group(array, bits_of):
        return lax.ppermute(array, "group", [(i, i ^ bits_of(i)) for i in range(groups)])

    def swap_core(array):
        return swap_group(array, lambda i: core_bit)

    def first_bit(i):
        return y_bit if i & core_bit else x_bit

    def second_bit(i):
        return x_bit if i & core_bit else y_bit

    gain = norm_gain.reshape(1, -1)
    def terms(which, dtypes, lifts, lifts_here):
        return partial_terms(
            which, dtypes, doc_lengths, key_grad, value_grad, rope_grad, *lifts,
            latent, gain, share, kva - latent.shape[1], block, lifts_here,
        )

    p3, *lifts = terms((3,), (BF16,), (key_lift, value_lift), False)
    got3 = swap_head(p3, 1)
    p2, p1 = terms((2, 1), (F32, BF16), lifts, True)
    (pair2,) = add_rows((p2, got3), (0, 0), [(kva, BF16)])
    pair2, p1, hidden, *lifts = lax.optimization_barrier((pair2, p1, hidden, *lifts))
    got2 = swap_head(pair2, 2)
    got1 = swap_head(p1, 1)
    sibling_hidden = swap_core(hidden)
    (p0,) = terms((0,), (F32,), lifts, True)
    ahead, rest = 2 * block, kva - 2 * block
    (q0_a,) = add_rows((p0, got1, got2), (0, 0, 0), [(ahead, BF16)])
    (q0_b,) = add_rows((p0, got1, got2), (ahead,) * 3, [(rest, BF16)], (q0_a,))
    q2_a, q2_b = swap_head(q0_a, 2), swap_head(q0_b, 2)
    even_a = stack((q0_a, q2_a))
    odd_a = swap_head(even_a, 1)
    q1_b = swap_head(stack((q0_b,), even_a, cost=SHORT), 1)
    q2_b = stack((q2_b,), even_a)
    q3_b = swap_head(q2_b, 1)
    odd_a = stack((odd_a,), q2_b, cost=MEDIUM)
    even_b = stack((q0_b, q2_b), cost=SHORT)

    def weights(even, odd, dtypes):
        shares = (even, odd) * 2 + (swap_core(even), swap_core(odd)) * 2
        half = even.shape[0] // 2
        return weight_terms(shares, (0, 0, half, half) * 2, hidden, sibling_hidden, block, dtypes)

    (for_both,) = weights(even_a, odd_a, (BF16,))
    got_both = swap_group(for_both, first_bit)
    odd_b = stack((q1_b, q3_b), for_both)
    for_first, for_second, mine = weights(even_b, odd_b, (BF16, F32, F32))
    got_first = swap_group(for_first, first_bit)
    kva_rows = natural_rows((even_a, odd_a, even_b, odd_b), block)
    (to_second,) = add_rows((for_second, got_both), (0, 0), [(block, BF16)], (kva_rows,))
    got_second = swap_group(to_second, second_bit)
    kva_rows, to_second = after(kva_rows, to_second)
    hidden_grad = hidden_terms(kva_rows, down_proj.T)
    weight_grad = mine + got_first.astype(F32) + got_second.astype(F32)
    return (hidden_grad, weight_grad)


def solution(mesh):
    shape = dict(mesh.shape)
    paired = shape["head"] == 4 and shape["group"] == 8
    return jax.shard_map(
        on_device if paired else on_device_any,
        mesh=mesh,
        in_specs=(
            P("group", "head"),
            P("group", "head"),
            P("group", "head"),
            P(None, "head"),
            P(None, "head"),
            P("group", None),
            P(),
            P("group", None),
            P("group", "head"),
            P("head", None),
        ),
        out_specs=(P("group", "head"), P("group", "head")),
        check_vma=False,
    )
```
